512 devices in a mesh: dp: 16 (over z), feat: 32 (over y, x, core).
Axes of the slice: x: 4, y: 4, z: 16, core: 2. Of those that a mesh axis runs over, the one named last changes fastest.
Arguments:
- features: bfloat16 [128, 65536], P('feat', 'dp'), may hold values from -6 to 6
- neighbours_one: int32 [65536, 15], P('dp'), may hold values from 0 to 4095
- counts_one: int32 [65536], P('dp'), may hold values from 1 to 15
- neighbours_two: int32 [65536, 10], P(('dp', 'feat')), may hold values from 0 to 4095, as said below
- counts_two: int32 [65536], P(('dp', 'feat')), may hold values from 1 to 10
- self_one: bfloat16 [128, 256], P('feat'), may hold values from -0.5 to 0.5
- neigh_one: bfloat16 [128, 256], P('feat'), may hold values from -1 to 1
- bias_one: float32 [256], replicated, may hold values from -3 to 3
- self_two: bfloat16 [256, 256], replicated, may hold values from -0.375 to 0.375
- neigh_two: bfloat16 [256, 256], replicated, may hold values from -0.5 to 0.5
- bias_two: float32 [256], replicated, may hold values from -3 to 3
- cotangent: bfloat16 [65536, 256], P(('dp', 'feat')), may hold values from -40 to 40
Outputs:
- hidden_two: bfloat16 [65536, 256], P(('dp', 'feat'))
- grad_self: float32 [256, 256], replicated
- grad_neigh: float32 [256, 256], replicated
- grad_bias: float32 [256], replicated
The draws below stay inside these ranges and needn't reach their ends.
Inputs may be any that keep to these rules, and one draw needn't show every extreme that they name: `neighbours_two`: the neighbours of node number k of a mini-batch lie in its own block of 128 nodes (k // 128) or in the block just before or just after it.
All inputs are finite; a program needn't handle non-finite values.
Results may differ from the reference program's by a relative error of at most 0.0053.
Values may be sent and summed in bfloat16 or wider, within the bound.
No kernel may reach another device: no remote copies, remote signals or barrier semaphores. Data moves between devices by JAX's collectives and lax.ppermute only.
A program may use at most 64 MiB of HBM per device.

```python
import jax
import jax.numpy as jnp
from jax import lax

FEATS = 128
HID = 256
FAN1 = 15
FAN2 = 10
NODE_DEV = 128
NODES = 4096
ALLNODES = 65536


def draw_neighbours_two(key, part):
    key = jax.random.fold_in(key, 11)
    first_key, second_key = jax.random.split(key)
    blocks = NODES // NODE_DEV
    number = jnp.arange(ALLNODES, dtype=jnp.int32) % NODES
    block = number // NODE_DEV
    offset = jax.random.randint(first_key, (ALLNODES, FAN2), -1, 2)
    target = jnp.clip(block[:, None] + offset, 0, blocks - 1)
    within = jax.random.randint(second_key, (ALLNODES, FAN2), 0, NODE_DEV)
    return (target * NODE_DEV + within).astype(jnp.int32)


def draw_cotangent(key, part):
    key = jax.random.fold_in(key, 23)
    first_key, second_key, third_key = jax.random.split(key, 3)
    block_count = ALLNODES // NODE_DEV
    noise = jnp.clip(jax.random.normal(first_key, (ALLNODES, HID), jnp.float32), -6.0, 6.0)
    shift = jax.random.uniform(second_key, (HID,), jnp.float32, -6.0, 6.0)
    signs = 2.0 * jax.random.randint(third_key, (block_count,), 0, 2).astype(jnp.float32) - 1.0
    row_sign = jnp.repeat(signs, NODE_DEV)
    ramp = 1.0 + 2.0 * jnp.arange(ALLNODES, dtype=jnp.float32) / (ALLNODES - 1)
    return (ramp[:, None] * (row_sign[:, None] * shift[None, :] + noise)).astype(jnp.bfloat16)


def with_ends(drawn, stream_key, low, largest):
    index_at = [jax.random.randint(jax.random.fold_in(stream_key, axis), (), 0, length) for axis, length in enumerate(drawn.shape)]
    longest = drawn.shape.index(max(drawn.shape))
    beside = index_at[:longest] + [(index_at[longest] + 1) % drawn.shape[longest]] + index_at[longest + 1:]
    return drawn.at[tuple(index_at)].set(low).at[tuple(beside)].set(largest)


def block_levels(own_key, shape, cuts, smallest, top_value):
    factor_of, own = 1.0, jax.random.fold_in(own_key, 6)
    for axis_at, blocks in cuts:
        heights = jnp.exp(jax.random.uniform(jax.random.fold_in(own, axis_at), (blocks,), jnp.float32, smallest / len(cuts), top_value / len(cuts)))
        factor_of = factor_of * jnp.repeat(heights, shape[axis_at] // blocks).reshape([-1 if axis == axis_at else 1 for axis in range(len(shape))])
    return factor_of


def bell_draw(key, extent, spread, bound, shards=(), held_as=jnp.bfloat16):
    factor_of = block_levels(key, extent, shards, -0.22, 0.18) if shards else 1.0
    drawn = jax.random.normal(key, extent, jnp.float32) * spread * factor_of
    return jnp.minimum(jnp.maximum(drawn, -bound), bound).astype(held_as)


def setup_inputs(seed: int = 0) -> dict:
    key_of = jax.random.split(jax.random.key(seed), 13)
    return {
        "features": bell_draw(key_of[0], (FEATS, ALLNODES), 1.0, 6.0, ((0, 32), (1, 16))),
        "neighbours_one": with_ends(jax.random.randint(key_of[1], (ALLNODES, FAN1), 0, NODES), jax.random.fold_in(key_of[1], 1), 0, NODES - 1).astype(jnp.int32),
        "counts_one": with_ends(jax.random.randint(key_of[2], (ALLNODES,), 1, FAN1 + 1), jax.random.fold_in(key_of[2], 1), 1, FAN1).astype(jnp.int32),
        "neighbours_two": draw_neighbours_two(jax.random.fold_in(key_of[12], 71), 0),
        "counts_two": with_ends(jax.random.randint(key_of[4], (ALLNODES,), 1, FAN2 + 1), jax.random.fold_in(key_of[4], 1), 1, FAN2).astype(jnp.int32),
        "self_one": bell_draw(key_of[5], (FEATS, HID), FEATS ** -0.5, 0.5, ((0, 32),)),
        "neigh_one": bell_draw(key_of[6], (FEATS, HID), (FEATS // 4) ** -0.5, 1.0, ((0, 32),)),
        "bias_one": bell_draw(key_of[7], (HID,), 0.5, 3.0, (), jnp.float32),
        "self_two": bell_draw(key_of[8], (HID, HID), HID ** -0.5, 0.375),
        "neigh_two": bell_draw(key_of[9], (HID, HID), (HID // 2) ** -0.5, 0.5),
        "bias_two": bell_draw(key_of[10], (HID,), 0.5, 3.0, (), jnp.float32),
        "cotangent": draw_cotangent(jax.random.fold_in(key_of[12], 71), 0),
    }


def neighbour_mean(table, neighbours, counts, fan):
    rows = table[neighbours].astype(jnp.float32)
    live = (jnp.arange(fan, dtype=jnp.int32)[None, :] < counts[:, None]).astype(jnp.float32)
    total = lax.optimization_barrier(jnp.sum(rows * live[:, :, None], axis=1))
    return total / counts[:, None].astype(jnp.float32)

def reference(features, neighbours_one, counts_one, neighbours_two, counts_two, self_one, neigh_one, bias_one, self_two, neigh_two, bias_two, cotangent):
    replicas = ALLNODES // NODES
    stacked_x = jnp.transpose(features.reshape(FEATS, replicas, NODES), (1, 2, 0))

    def one_batch(pieces):
        node_x, first_ids, first_counts, second_ids, second_counts, grad_out = pieces
        agg_one = neighbour_mean(node_x, first_ids, first_counts, FAN1).astype(jnp.bfloat16)
        pre_one = jnp.dot(node_x, self_one, preferred_element_type=jnp.float32) + jnp.dot(agg_one, neigh_one, preferred_element_type=jnp.float32) + bias_one
        hidden_one = jax.nn.gelu(pre_one, approximate=True).astype(jnp.bfloat16)
        agg_two = neighbour_mean(hidden_one, second_ids, second_counts, FAN2).astype(jnp.bfloat16)
        pre_two = jnp.dot(hidden_one, self_two, preferred_element_type=jnp.float32) + jnp.dot(agg_two, neigh_two, preferred_element_type=jnp.float32) + bias_two
        hidden_two = jax.nn.gelu(pre_two, approximate=True).astype(jnp.bfloat16)
        slope_fn = jax.vjp(lambda value: jax.nn.gelu(value, approximate=True), pre_two)[1]
        delta = slope_fn(grad_out.astype(jnp.float32))[0].astype(jnp.bfloat16)
        grad_s = jnp.dot(hidden_one.T, delta, preferred_element_type=jnp.float32)
        grad_n = jnp.dot(agg_two.T, delta, preferred_element_type=jnp.float32)
        grad_b = lax.optimization_barrier(jnp.sum(delta.astype(jnp.float32), axis=0))
        return (hidden_two, grad_s, grad_n, grad_b)
    outputs = lax.map(one_batch, (stacked_x, neighbours_one.reshape(replicas, NODES, FAN1), counts_one.reshape(replicas, NODES), neighbours_two.reshape(replicas, NODES, FAN2), counts_two.reshape(replicas, NODES), cotangent.reshape(replicas, NODES, HID)))
    hidden_two = outputs[0].reshape(ALLNODES, HID)
    scale = 1.0 / ALLNODES
    grad_self = lax.optimization_barrier(jnp.sum(outputs[1], axis=0)) * scale
    grad_neigh = lax.optimization_barrier(jnp.sum(outputs[2], axis=0)) * scale
    grad_bias = lax.optimization_barrier(jnp.sum(outputs[3], axis=0)) * scale
    return (hidden_two, grad_self, grad_neigh, grad_bias)
```

```python
import functools
import math

import jax
import jax.numpy as jnp
from jax import lax
from jax.experimental import pallas as pl
from jax.experimental.pallas import tpu as pltpu
from jax.sharding import Mesh
from jax.sharding import PartitionSpec as P

LANES = 128
INNER = math.sqrt(2.0 / math.pi)
CUBIC = 0.044715
VMEM_BYTES = 48 * 1024 * 1024


def pick_kernel(feats_ref, ids_ref, counts_ref, self_ref, neigh_ref, out_ref, table, sums):
    rows, nodes = feats_ref.shape
    fan = ids_ref.shape[0]
    blocks = nodes // LANES
    wide = feats_ref[...].astype(jnp.float32)
    table[0:rows, :] = wide
    table[rows : 2 * rows, :] = wide
    upper = lax.broadcasted_iota(jnp.int32, (2 * rows, LANES), 0) < rows

    def two_blocks(pair, carry):
        start = pl.multiple_of(pair * 2 * LANES, 2 * LANES)
        first, second = pl.ds(start, LANES), pl.ds(start + LANES, LANES)

        def both(ref, k):
            return jnp.where(
                upper,
                jnp.broadcast_to(ref[k : k + 1, first], upper.shape),
                jnp.broadcast_to(ref[k : k + 1, second], upper.shape),
            )

        counts = both(counts_ref, 0)
        total = jnp.zeros(upper.shape, jnp.float32)
        for k in range(fan):
            ids = both(ids_ref, k)
            lane = jnp.bitwise_and(ids, LANES - 1)
            block = lax.shift_right_logical(ids, 7)
            level = [
                jnp.take_along_axis(
                    table[:, j * LANES : (j + 1) * LANES], lane, axis=1, mode="promise_in_bounds"
                )
                for j in range(blocks)
            ]
            bit = 1
            while len(level) > 1:
                odd = jnp.bitwise_and(block, bit) != 0
                level = [
                    jnp.where(odd, level[i + 1], level[i]) for i in range(0, len(level), 2)
                ]
                bit *= 2
            total = total + jnp.where(counts > k, level[0], 0.0)
        mean = total / counts.astype(jnp.float32)
        at_first = pl.multiple_of(start + LANES, LANES)
        at_second = pl.multiple_of(start + 2 * LANES, LANES)
        sums[:, pl.ds(at_first, LANES)] = jnp.where(
            upper, table[:, first], pltpu.roll(mean, rows, axis=0)
        )
        sums[:, pl.ds(at_second, LANES)] = jnp.where(upper, table[:, second], mean)
        return carry

    lax.fori_loop(0, blocks // 2, two_blocks, 0)
    sums[:, 0:LANES] = sums[:, blocks * LANES : (blocks + 1) * LANES]
    sums[:, (blocks + 1) * LANES :] = sums[:, LANES : 2 * LANES]
    weights = jnp.concatenate(
        [self_ref[...].astype(jnp.float32), neigh_ref[...].astype(jnp.float32)], axis=0
    ).astype(jnp.bfloat16)
    for block in range(blocks):
        out_ref[block, :, 0 : 3 * LANES] = sums[
            :, block * LANES : (block + 3) * LANES
        ].astype(jnp.bfloat16)
        out_ref[block, :, 3 * LANES :] = weights


def gelu_parts(value):
    square = value * value
    bent = jnp.tanh(INNER * (value + CUBIC * (value * square)))
    half = 0.5 * (1.0 + bent)
    slope = half + 0.5 * value * (1.0 - bent * bent) * (INNER * (1.0 + 3.0 * CUBIC * square))
    return value * half, slope


def layers_kernel(
    got_ref, ids_ref, counts_ref, bias_one_ref, self_ref, neigh_ref, bias_two_ref, cot_ref,
    hidden_ref, grads_ref, bias_ref,
):
    node_rows = cot_ref.shape[0]
    hid = cot_ref.shape[1]
    span = 3 * node_rows
    fan = ids_ref.shape[1]
    over_rows = (((0,), (0,)), ((), ()))
    got = got_ref[...]
    pre_one = lax.dot_general(
        got[:, :span], got[:, span:], over_rows, preferred_element_type=jnp.float32
    )
    hidden = gelu_parts(pre_one + bias_one_ref[...])[0].astype(jnp.bfloat16)
    own = hidden[node_rows : 2 * node_rows]
    ids, counts = ids_ref[...], counts_ref[...]
    column = lax.broadcasted_iota(jnp.int32, (node_rows, span), 1)
    often = jnp.zeros((node_rows, span), jnp.float32)
    for k in range(fan):
        hit = jnp.where(counts > k, ids[:, k : k + 1], -1) == column
        often = often + jnp.where(hit, 1.0, 0.0)
    summed = jnp.dot(often.astype(jnp.bfloat16), hidden, preferred_element_type=jnp.float32)
    agg = (summed / counts.astype(jnp.float32)).astype(jnp.bfloat16)
    pre_two = jnp.dot(own, self_ref[...], preferred_element_type=jnp.float32)
    pre_two = pre_two + jnp.dot(agg, neigh_ref[...], preferred_element_type=jnp.float32)
    value, slope = gelu_parts(pre_two + bias_two_ref[...])
    hidden_ref[...] = value.astype(jnp.bfloat16)
    delta = (cot_ref[...].astype(jnp.float32) * slope).astype(jnp.bfloat16)
    grads_ref[0:hid, :] = lax.dot_general(
        own, delta, over_rows, preferred_element_type=jnp.float32
    )
    grads_ref[hid:, :] = lax.dot_general(
        agg, delta, over_rows, preferred_element_type=jnp.float32
    )
    bias_ref[...] = jnp.sum(delta.astype(jnp.float32), axis=0, keepdims=True)


def local(
    features,
    neighbours_one,
    counts_one,
    neighbours_two,
    counts_two,
    self_one,
    neigh_one,
    bias_one,
    self_two,
    neigh_two,
    bias_two,
    cotangent,
):
    rows, batch_nodes = features.shape
    groups = lax.axis_size("feat")
    node_rows = batch_nodes // groups
    hid = self_one.shape[1]
    span = 3 * node_rows
    params = pltpu.CompilerParams(vmem_limit_bytes=VMEM_BYTES)
    chunks = pl.pallas_call(
        pick_kernel,
        out_shape=jax.ShapeDtypeStruct((groups, 2 * rows, span + hid), jnp.bfloat16),
        scratch_shapes=[
            pltpu.VMEM((2 * rows, batch_nodes), jnp.float32),
            pltpu.VMEM((2 * rows, batch_nodes + 2 * node_rows), jnp.float32),
        ],
        compiler_params=params,
        name="pick",
    )(features, neighbours_one.T, counts_one[None, :], self_one, neigh_one)
    got = lax.all_to_all(chunks, "feat", 0, 0, tiled=True)
    first_node = lax.axis_index("feat") * node_rows
    hidden_two, grads, bias = pl.pallas_call(
        layers_kernel,
        out_shape=(
            jax.ShapeDtypeStruct((node_rows, hid), jnp.bfloat16),
            jax.ShapeDtypeStruct((2 * hid, hid), jnp.float32),
            jax.ShapeDtypeStruct((1, hid), jnp.float32),
        ),
        compiler_params=params,
        name="layers",
    )(
        got.reshape(groups * 2 * rows, span + hid),
        neighbours_two - first_node + node_rows,
        counts_two[:, None],
        bias_one[None, :],
        self_two,
        neigh_two,
        bias_two[None, :],
        cotangent,
    )
    group = lax.axis_size("pair") * groups
    others = lax.axis_size("apart")
    parts = jnp.concatenate(
        [grads.reshape(group, -1, 2, LANES), bias.reshape(1, 1, 2, LANES) * jnp.ones((group, 1, 1, 1), jnp.float32)], axis=1
    )
    inner = lax.all_to_all(parts, ("pair", "feat"), 0, 0, tiled=True).sum(axis=0)
    spread = jnp.broadcast_to(inner[None], (others,) + inner.shape)
    total = lax.all_to_all(spread, "apart", 0, 0, tiled=True).sum(axis=0)
    scale = 1.0 / (batch_nodes * lax.axis_size("pair") * others)
    total = total * scale
    total_bias = total[-1].reshape(hid)
    narrow = total[:-1].astype(jnp.bfloat16)
    spread = jnp.broadcast_to(narrow[None], (group,) + narrow.shape)
    whole = lax.all_to_all(spread, ("pair", "feat"), 0, 0, tiled=True)
    whole = whole.reshape(2 * hid, hid).astype(jnp.float32)
    return hidden_two, whole[:hid], whole[hid:], total_bias


def solution(mesh):
    replicas, groups = mesh.devices.shape
    split = Mesh(mesh.devices.reshape(replicas // 2, 2, groups), ("apart", "pair", "feat"))
    dp = ("apart", "pair")
    every = ("apart", "pair", "feat")
    return jax.shard_map(
        local,
        mesh=split,
        in_specs=(
            P("feat", dp),
            P(dp, None),
            P(dp),
            P(every, None),
            P(every),
            P("feat", None),
            P("feat", None),
            P(),
            P(),
            P(),
            P(),
            P(every, None),
        ),
        out_specs=(P(every, None), P(), P(), P()),
        check_vma=False,
    )
```

```python
import functools
import math

import jax
import jax.numpy as jnp
from jax import lax
from jax.experimental import pallas as pl
from jax.experimental.pallas import tpu as pltpu
from jax.sharding import Mesh
from jax.sharding import PartitionSpec as P

LANES = 128
INNER = math.sqrt(2.0 / math.pi)
CUBIC = 0.044715
VMEM_BYTES = 48 * 1024 * 1024
PICK_VMEM_BYTES = 57_000_000


WITHIN = lax.GatherDimensionNumbers(
    offset_dims=(),
    collapsed_slice_dims=(1,),
    start_index_map=(1,),
    operand_batching_dims=(0,),
    start_indices_batching_dims=(0,),
)


def lane_gather(table, lane):
    return lax.gather(
        table, lane[..., None], WITHIN, (1, 1), mode=lax.GatherScatterMode.PROMISE_IN_BOUNDS
    )


def pick_kernel(
    feats_hbm, ids_hbm, counts_hbm, self_hbm, neigh_hbm, out_ref,
    feats_ref, ids_ref, counts_ref, self_ref, neigh_ref, wide, table, sums, arrived,
):
    copies = [
        pltpu.make_async_copy(source, target, arrived.at[i])
        for i, (source, target) in enumerate(
            (
                (feats_hbm, feats_ref),
                (ids_hbm, ids_ref),
                (counts_hbm, counts_ref),
                (self_hbm, self_ref),
                (neigh_hbm, neigh_ref),
            )
        )
    ]
    for copy in copies:
        copy.start()
    rows, nodes = feats_ref.shape
    fan = ids_ref.shape[0]
    blocks = nodes // LANES
    copies[0].wait()
    values = feats_ref[...].astype(jnp.float32)
    wide[0:rows, :] = values
    wide[rows : 2 * rows, :] = values
    table[...] = jnp.concatenate([wide[...]] * 2, axis=0).astype(jnp.bfloat16)
    for copy in copies[1:]:
        copy.wait()
    row = lax.broadcasted_iota(jnp.int32, (4 * rows, LANES), 0)
    upper = lax.broadcasted_iota(jnp.int32, (2 * rows, LANES), 0) < rows

    def four_blocks(quad, carry):
        start = pl.multiple_of(quad * 4 * LANES, 4 * LANES)

        def spread(ref, k):
            parts = [
                jnp.broadcast_to(ref[k : k + 1, pl.ds(start + i * LANES, LANES)], row.shape)
                for i in range(4)
            ]
            return jnp.where(
                row < 2 * rows,
                jnp.where(row < rows, parts[0], parts[1]),
                jnp.where(row < 3 * rows, parts[2], parts[3]),
            )

        counts = spread(counts_ref, 0)
        total = jnp.zeros(row.shape, jnp.float32)
        for k in range(fan):
            ids = spread(ids_ref, k)
            lane = jnp.bitwise_and(ids, LANES - 1).astype(jnp.int16)
            block = lax.shift_right_logical(ids, 7).astype(jnp.int16)
            level = [
                lane_gather(table[:, j * LANES : (j + 1) * LANES], lane) for j in range(blocks)
            ]
            bit = 1
            while len(level) > 1:
                odd = jnp.bitwise_and(block, jnp.int16(bit)) != 0
                level = [
                    jnp.where(odd, level[i + 1], level[i]) for i in range(0, len(level), 2)
                ]
                bit *= 2
            total = total + jnp.where(counts > k, level[0].astype(jnp.float32), 0.0)
        mean = total / counts.astype(jnp.float32)
        for i in range(4):
            half = mean[(i // 2) * 2 * rows : (i // 2 + 1) * 2 * rows]
            if i % 2 == 0:
                half = pltpu.roll(half, rows, axis=0)
            to = pl.multiple_of(start + (i + 1) * LANES, LANES)
            sums[:, pl.ds(to, LANES)] = jnp.where(
                upper, wide[:, pl.ds(start + i * LANES, LANES)], half
            )
        return carry

    lax.fori_loop(0, blocks // 4, four_blocks, 0)
    sums[:, 0:LANES] = sums[:, blocks * LANES : (blocks + 1) * LANES]
    sums[:, (blocks + 1) * LANES :] = sums[:, LANES : 2 * LANES]
    weights = jnp.concatenate(
        [self_ref[...].astype(jnp.float32), neigh_ref[...].astype(jnp.float32)], axis=0
    ).astype(jnp.bfloat16)
    for block in range(blocks):
        out_ref[block, :, 0 : 3 * LANES] = sums[
            :, block * LANES : (block + 3) * LANES
        ].astype(jnp.bfloat16)
        out_ref[block, :, 3 * LANES :] = weights


def gelu_parts(value):
    square = value * value
    bent = jnp.tanh(INNER * (value + CUBIC * (value * square)))
    half = 0.5 * (1.0 + bent)
    slope = half + 0.5 * value * (1.0 - bent * bent) * (INNER * (1.0 + 3.0 * CUBIC * square))
    return value * half, slope


def layers_kernel(
    got_ref, ids_ref, counts_ref, bias_one_ref, self_ref, neigh_ref, bias_two_ref, cot_ref,
    hidden_ref, grads_ref, bias_ref,
):
    node_rows = cot_ref.shape[0]
    hid = cot_ref.shape[1]
    span = 3 * node_rows
    fan = ids_ref.shape[1]
    over_rows = (((0,), (0,)), ((), ()))
    got = got_ref[...]
    pre_one = lax.dot_general(
        got[:, :span], got[:, span:], over_rows, preferred_element_type=jnp.float32
    )
    hidden = gelu_parts(pre_one + bias_one_ref[...])[0].astype(jnp.bfloat16)
    own = hidden[node_rows : 2 * node_rows]
    ids, counts = ids_ref[...], counts_ref[...]
    column = lax.broadcasted_iota(jnp.int32, (node_rows, span), 1)
    often = jnp.zeros((node_rows, span), jnp.float32)
    for k in range(fan):
        hit = jnp.where(counts > k, ids[:, k : k + 1], -1) == column
        often = often + jnp.where(hit, 1.0, 0.0)
    summed = jnp.dot(often.astype(jnp.bfloat16), hidden, preferred_element_type=jnp.float32)
    agg = (summed / counts.astype(jnp.float32)).astype(jnp.bfloat16)
    pre_two = jnp.dot(own, self_ref[...], preferred_element_type=jnp.float32)
    pre_two = pre_two + jnp.dot(agg, neigh_ref[...], preferred_element_type=jnp.float32)
    value, slope = gelu_parts(pre_two + bias_two_ref[...])
    hidden_ref[...] = value.astype(jnp.bfloat16)
    delta = (cot_ref[...].astype(jnp.float32) * slope).astype(jnp.bfloat16)
    grads_ref[0:hid, :] = lax.dot_general(
        own, delta, over_rows, preferred_element_type=jnp.float32
    )
    grads_ref[hid:, :] = lax.dot_general(
        agg, delta, over_rows, preferred_element_type=jnp.float32
    )
    bias_ref[...] = jnp.sum(delta.astype(jnp.float32), axis=0, keepdims=True)


def local(
    features,
    neighbours_one,
    counts_one,
    neighbours_two,
    counts_two,
    self_one,
    neigh_one,
    bias_one,
    self_two,
    neigh_two,
    bias_two,
    cotangent,
):
    rows, batch_nodes = features.shape
    groups = lax.axis_size("feat")
    node_rows = batch_nodes // groups
    hid = self_one.shape[1]
    span = 3 * node_rows
    params = pltpu.CompilerParams(vmem_limit_bytes=VMEM_BYTES)
    chunks = pl.pallas_call(
        pick_kernel,
        out_shape=jax.ShapeDtypeStruct((groups, 2 * rows, span + hid), jnp.bfloat16),
        in_specs=[pl.BlockSpec(memory_space=pltpu.HBM)] * 5,
        scratch_shapes=[
            pltpu.VMEM(features.shape, features.dtype),
            pltpu.VMEM(neighbours_one.shape[::-1], jnp.int32),
            pltpu.VMEM((1, batch_nodes), jnp.int32),
            pltpu.VMEM(self_one.shape, self_one.dtype),
            pltpu.VMEM(neigh_one.shape, neigh_one.dtype),
            pltpu.VMEM((2 * rows, batch_nodes), jnp.float32),
            pltpu.VMEM((4 * rows, batch_nodes), jnp.bfloat16),
            pltpu.VMEM((2 * rows, batch_nodes + 2 * node_rows), jnp.float32),
            pltpu.SemaphoreType.DMA((5,)),
        ],
        compiler_params=pltpu.CompilerParams(vmem_limit_bytes=PICK_VMEM_BYTES),
        name="pick",
    )(features, neighbours_one.T, counts_one[None, :], self_one, neigh_one)
    got = lax.all_to_all(chunks, "feat", 0, 0, tiled=True)
    first_node = lax.axis_index("feat") * node_rows
    hidden_two, grads, bias = pl.pallas_call(
        layers_kernel,
        out_shape=(
            jax.ShapeDtypeStruct((node_rows, hid), jnp.bfloat16),
            jax.ShapeDtypeStruct((2 * hid, hid), jnp.float32),
            jax.ShapeDtypeStruct((1, hid), jnp.float32),
        ),
        compiler_params=params,
        name="layers",
    )(
        got.reshape(groups * 2 * rows, span + hid),
        neighbours_two - first_node + node_rows,
        counts_two[:, None],
        bias_one[None, :],
        self_two,
        neigh_two,
        bias_two[None, :],
        cotangent,
    )
    group = lax.axis_size("pair") * groups
    others = lax.axis_size("apart")
    parts = jnp.concatenate(
        [grads.reshape(group, -1, 2, LANES), bias.reshape(1, 1, 2, LANES) * jnp.ones((group, 1, 1, 1), jnp.float32)], axis=1
    )
    inner = lax.all_to_all(parts, ("pair", "feat"), 0, 0, tiled=True).sum(axis=0)
    spread = jnp.broadcast_to(inner[None], (others,) + inner.shape)
    total = lax.all_to_all(spread, "apart", 0, 0, tiled=True).sum(axis=0)
    scale = 1.0 / (batch_nodes * lax.axis_size("pair") * others)
    total = total * scale
    total_bias = total[-1].reshape(hid)
    narrow = total[:-1].astype(jnp.bfloat16)
    spread = jnp.broadcast_to(narrow[None], (group,) + narrow.shape)
    whole = lax.all_to_all(spread, ("pair", "feat"), 0, 0, tiled=True)
    whole = whole.reshape(2 * hid, hid).astype(jnp.float32)
    return hidden_two, whole[:hid], whole[hid:], total_bias


def solution(mesh):
    replicas, groups = mesh.devices.shape
    split = Mesh(mesh.devices.reshape(replicas // 2, 2, groups), ("apart", "pair", "feat"))
    dp = ("apart", "pair")
    every = ("apart", "pair", "feat")
    return jax.shard_map(
        local,
        mesh=split,
        in_specs=(
            P("feat", dp),
            P(dp, None),
            P(dp),
            P(every, None),
            P(every),
            P("feat", None),
            P("feat", None),
            P(),
            P(),
            P(),
            P(),
            P(every, None),
        ),
        out_specs=(P(every, None), P(), P(), P()),
        check_vma=False,
    )
```

```python
import math

import jax
import jax.numpy as jnp
from jax import lax
from jax.experimental import pallas as pl
from jax.experimental.pallas import tpu as pltpu
from jax.sharding import Mesh
from jax.sharding import PartitionSpec as P

LANES = 128
INNER = math.sqrt(2.0 / math.pi)
CUBIC = 0.044715
VMEM_BYTES = 48 * 1024 * 1024
PICK_VMEM_BYTES = 57_000_000


WITHIN = lax.GatherDimensionNumbers(
    offset_dims=(),
    collapsed_slice_dims=(1,),
    start_index_map=(1,),
    operand_batching_dims=(0,),
    start_indices_batching_dims=(0,),
)


def lane_gather(table, lane):
    return lax.gather(
        table, lane[..., None], WITHIN, (1, 1), mode=lax.GatherScatterMode.PROMISE_IN_BOUNDS
    )


def pick_kernel(
    feats_hbm, ids_hbm, counts_hbm, self_hbm, neigh_hbm, out_ref,
    feats_ref, ids_ref, counts_ref, self_ref, neigh_ref, wide, table, sums, arrived,
):
    copies = [
        pltpu.make_async_copy(source, target, arrived.at[i])
        for i, (source, target) in enumerate(
            (
                (feats_hbm, feats_ref),
                (ids_hbm, ids_ref),
                (counts_hbm, counts_ref),
                (self_hbm, self_ref),
                (neigh_hbm, neigh_ref),
            )
        )
    ]
    for copy in copies:
        copy.start()
    rows, nodes = feats_ref.shape
    fan = ids_ref.shape[0]
    blocks = nodes // LANES
    copies[0].wait()
    values = feats_ref[...].astype(jnp.float32)
    wide[0:rows, :] = values
    wide[rows : 2 * rows, :] = values
    table[...] = jnp.concatenate([wide[...]] * 2, axis=0).astype(jnp.bfloat16)
    for copy in copies[1:]:
        copy.wait()
    row = lax.broadcasted_iota(jnp.int32, (4 * rows, LANES), 0)
    upper = lax.broadcasted_iota(jnp.int32, (2 * rows, LANES), 0) < rows

    def four_blocks(quad, carry):
        start = pl.multiple_of(quad * 4 * LANES, 4 * LANES)

        def spread(ref, k):
            parts = [
                jnp.broadcast_to(ref[k : k + 1, pl.ds(start + i * LANES, LANES)], row.shape)
                for i in range(4)
            ]
            return jnp.where(
                row < 2 * rows,
                jnp.where(row < rows, parts[0], parts[1]),
                jnp.where(row < 3 * rows, parts[2], parts[3]),
            )

        counts = spread(counts_ref, 0)
        total = jnp.zeros(row.shape, jnp.float32)
        for k in range(fan):
            ids = spread(ids_ref, k)
            lane = jnp.bitwise_and(ids, LANES - 1).astype(jnp.int16)
            block = lax.shift_right_logical(ids, 7).astype(jnp.int16)
            level = [
                lane_gather(table[:, j * LANES : (j + 1) * LANES], lane) for j in range(blocks)
            ]
            bit = 1
            while len(level) > 1:
                odd = jnp.bitwise_and(block, jnp.int16(bit)) != 0
                level = [
                    jnp.where(odd, level[i + 1], level[i]) for i in range(0, len(level), 2)
                ]
                bit *= 2
            total = total + jnp.where(counts > k, level[0].astype(jnp.float32), 0.0)
        mean = total / counts.astype(jnp.float32)
        for i in range(4):
            half = mean[(i // 2) * 2 * rows : (i // 2 + 1) * 2 * rows]
            if i % 2 == 0:
                half = pltpu.roll(half, rows, axis=0)
            to = pl.multiple_of(start + (i + 1) * LANES, LANES)
            sums[:, pl.ds(to, LANES)] = jnp.where(
                upper, wide[:, pl.ds(start + i * LANES, LANES)], half
            )
        return carry

    lax.fori_loop(0, blocks // 4, four_blocks, 0)
    sums[:, 0:LANES] = sums[:, blocks * LANES : (blocks + 1) * LANES]
    sums[:, (blocks + 1) * LANES :] = sums[:, LANES : 2 * LANES]
    weights = jnp.concatenate(
        [self_ref[...].astype(jnp.float32), neigh_ref[...].astype(jnp.float32)], axis=0
    ).astype(jnp.bfloat16)
    for first in range(0, blocks, 2):
        span = sums[:, first * LANES : (first + 4) * LANES].astype(jnp.bfloat16)
        for block in (first, first + 1):
            out_ref[block, :, 0 : 4 * LANES] = span
            out_ref[block, :, 4 * LANES :] = weights


def gelu_parts(value):
    square = value * value
    bent = jnp.tanh(INNER * (value + CUBIC * (value * square)))
    half = 0.5 * (1.0 + bent)
    slope = half + 0.5 * value * (1.0 - bent * bent) * (INNER * (1.0 + 3.0 * CUBIC * square))
    return value * half, slope


def layers_kernel(
    core_ref, got_ref, own_meta_ref, other_meta_ref, counts_ref, bias_ref, self_ref, neigh_ref,
    own_cot_ref, other_cot_ref, hidden_ref, grads_ref, bias_grad_ref,
):
    node_rows, hid = own_cot_ref.shape
    span = 4 * node_rows
    fan = own_meta_ref.shape[0]
    over_rows = (((0,), (0,)), ((), ()))
    is_first = core_ref[0] == 0
    got = got_ref[...]
    pre_one = lax.dot_general(
        got[:, :span], got[:, span:], over_rows, preferred_element_type=jnp.float32
    )
    hidden = gelu_parts(pre_one + bias_ref[0:1, :])[0].astype(jnp.bfloat16)
    own = hidden[node_rows : 3 * node_rows]
    own_meta, other_meta = own_meta_ref[...], other_meta_ref[...]
    number = lax.broadcasted_iota(jnp.int32, (span, node_rows), 0).astype(jnp.int16)
    one, zero = jnp.ones((), jnp.bfloat16), jnp.zeros((), jnp.bfloat16)
    often = []
    for meta in (
        jnp.where(is_first, own_meta, other_meta),
        jnp.where(is_first, other_meta, own_meta),
    ):
        total = jnp.zeros((span, node_rows), jnp.bfloat16)
        for k in range(fan):
            ids = jnp.broadcast_to(meta[k : k + 1, :], (span, node_rows)).astype(jnp.int16)
            total = total + jnp.where(ids == number, one, zero)
        often.append(total)
    summed = lax.dot_general(
        jnp.concatenate(often, axis=1), hidden, over_rows, preferred_element_type=jnp.float32
    )
    agg = (summed / counts_ref[...].astype(jnp.float32)).astype(jnp.bfloat16)
    pre_two = jnp.dot(own, self_ref[...], preferred_element_type=jnp.float32)
    pre_two = pre_two + jnp.dot(agg, neigh_ref[...], preferred_element_type=jnp.float32)
    value, slope = gelu_parts(pre_two + bias_ref[1:2, :])
    hidden_ref[...] = jnp.where(is_first, value[:node_rows], value[node_rows:]).astype(jnp.bfloat16)
    own_cot = own_cot_ref[...].astype(jnp.float32)
    other_cot = other_cot_ref[...].astype(jnp.float32)
    cot = jnp.concatenate(
        [jnp.where(is_first, own_cot, other_cot), jnp.where(is_first, other_cot, own_cot)], axis=0
    )
    delta = (cot * slope).astype(jnp.bfloat16)
    rows = jnp.where(is_first, own, agg)
    grads_ref[...] = lax.dot_general(rows, delta, over_rows, preferred_element_type=jnp.float32)
    bias_grad_ref[...] = jnp.sum(delta.astype(jnp.float32), axis=0, keepdims=True)


def repeat_kernel(part_ref, out_ref):
    part = part_ref[...].astype(jnp.bfloat16)
    for to in range(out_ref.shape[0]):
        out_ref[to] = part


def widen_kernel(got_ref, self_ref, neigh_ref):
    pairs, chips, _, rows, _ = got_ref.shape
    for pair in range(pairs):
        for chip in range(chips):
            at = (pair * chips + chip) * rows
            self_ref[at : at + rows, :] = got_ref[pair, chip, 0].astype(jnp.float32)
            neigh_ref[at : at + rows, :] = got_ref[pair, chip, 1].astype(jnp.float32)


def local(
    features,
    neighbours_one,
    counts_one,
    neighbours_two,
    counts_two,
    self_one,
    neigh_one,
    bias_one,
    self_two,
    neigh_two,
    bias_two,
    cotangent,
):
    rows, batch_nodes = features.shape
    pairs, chips, cores = lax.axis_size("pair"), lax.axis_size("chip"), lax.axis_size("core")
    others = lax.axis_size("apart")
    groups = chips * cores
    node_rows = batch_nodes // groups
    hid = self_one.shape[1]
    span = 4 * node_rows
    params = pltpu.CompilerParams(vmem_limit_bytes=VMEM_BYTES)
    chunks = pl.pallas_call(
        pick_kernel,
        out_shape=jax.ShapeDtypeStruct((groups, 2 * rows, span + hid), jnp.bfloat16),
        in_specs=[pl.BlockSpec(memory_space=pltpu.HBM)] * 5,
        scratch_shapes=[
            pltpu.VMEM(features.shape, features.dtype),
            pltpu.VMEM(neighbours_one.shape[::-1], jnp.int32),
            pltpu.VMEM((1, batch_nodes), jnp.int32),
            pltpu.VMEM(self_one.shape, self_one.dtype),
            pltpu.VMEM(neigh_one.shape, neigh_one.dtype),
            pltpu.VMEM((2 * rows, batch_nodes), jnp.float32),
            pltpu.VMEM((4 * rows, batch_nodes), jnp.bfloat16),
            pltpu.VMEM((2 * rows, batch_nodes + 2 * node_rows), jnp.float32),
            pltpu.SemaphoreType.DMA((5,)),
        ],
        compiler_params=pltpu.CompilerParams(vmem_limit_bytes=PICK_VMEM_BYTES),
        name="pick",
    )(features, neighbours_one.T, counts_one[None, :], self_one, neigh_one)
    got = lax.all_to_all(chunks, ("chip", "core"), 0, 0, tiled=True)

    swap = [(0, 1), (1, 0)]
    core = lax.axis_index("core")
    first_node = (lax.axis_index("chip") * cores - 1) * node_rows
    meta = jnp.concatenate([neighbours_two.T, counts_two[None, :]], axis=0)
    other_meta = lax.ppermute(meta, "core", swap)
    other_cot = lax.ppermute(cotangent, "core", swap)

    def numbers(kept):
        live = jnp.arange(kept.shape[0] - 1, dtype=jnp.int32)[:, None] < kept[-1:]
        return jnp.where(live, kept[:-1] - first_node, -1)

    counts = jnp.where(
        core == 0,
        jnp.concatenate([counts_two, other_meta[-1]]),
        jnp.concatenate([other_meta[-1], counts_two]),
    )
    hidden_two, grads, bias = pl.pallas_call(
        layers_kernel,
        out_shape=(
            jax.ShapeDtypeStruct((node_rows, hid), jnp.bfloat16),
            jax.ShapeDtypeStruct((hid, hid), jnp.float32),
            jax.ShapeDtypeStruct((1, hid), jnp.float32),
        ),
        in_specs=[pl.BlockSpec(memory_space=pltpu.SMEM)]
        + [pl.BlockSpec(memory_space=pltpu.VMEM)] * 9,
        compiler_params=params,
        name="layers",
    )(
        core[None],
        got.reshape(groups * 2 * rows, span + hid),
        numbers(meta),
        numbers(other_meta),
        counts[:, None],
        jnp.stack([bias_one, bias_two]),
        self_two,
        neigh_two,
        cotangent,
        other_cot,
    )
    group = pairs * chips
    parts = jnp.concatenate(
        [
            grads.reshape(group, -1, 2, LANES),
            jnp.broadcast_to(bias.reshape(1, 1, 2, LANES), (group, 1, 2, LANES)),
        ],
        axis=1,
    )
    inner = lax.all_to_all(parts, ("pair", "chip"), 0, 0, tiled=True).sum(axis=0)
    spread = jnp.broadcast_to(inner[None], (others,) + inner.shape)
    total = lax.all_to_all(spread, "apart", 0, 0, tiled=True).sum(axis=0)
    total = total * (1.0 / (batch_nodes * pairs * others))
    part = total[:-1].reshape(hid // group, hid)
    everyone = group * cores
    spread = pl.pallas_call(
        repeat_kernel,
        out_shape=jax.ShapeDtypeStruct((everyone,) + part.shape, jnp.bfloat16),
        compiler_params=params,
        name="repeat",
    )(part)
    whole = lax.all_to_all(spread, ("pair", "chip", "core"), 0, 0, tiled=True)
    grad_self, grad_neigh = pl.pallas_call(
        widen_kernel,
        out_shape=(jax.ShapeDtypeStruct((hid, hid), jnp.float32),) * 2,
        compiler_params=params,
        name="widen",
    )(whole.reshape((pairs, chips, cores) + part.shape))
    return hidden_two, grad_self, grad_neigh, total[-1].reshape(hid)


def solution(mesh):
    replicas, groups = mesh.devices.shape
    split = Mesh(
        mesh.devices.reshape(replicas // 2, 2, groups // 2, 2), ("apart", "pair", "chip", "core")
    )
    dp = ("apart", "pair")
    feat = ("chip", "core")
    every = dp + feat
    return jax.shard_map(
        local,
        mesh=split,
        in_specs=(
            P(feat, dp),
            P(dp, None),
            P(dp),
            P(every, None),
            P(every),
            P(feat, None),
            P(feat, None),
            P(),
            P(),
            P(),
            P(),
            P(every, None),
        ),
        out_specs=(P(every, None), P(), P(), P()),
        check_vma=False,
    )
```

```python
import functools
import math

import jax
import jax.numpy as jnp
from jax import lax
from jax.experimental import pallas as pl
from jax.experimental.pallas import tpu as pltpu
from jax.sharding import Mesh
from jax.sharding import PartitionSpec as P

LANES = 128
INNER = math.sqrt(2.0 / math.pi)
CUBIC = 0.044715
VMEM_BYTES = 48 * 1024 * 1024
PICK_VMEM_BYTES = 57_000_000


WITHIN = lax.GatherDimensionNumbers(
    offset_dims=(),
    collapsed_slice_dims=(1,),
    start_index_map=(1,),
    operand_batching_dims=(0,),
    start_indices_batching_dims=(0,),
)


def lane_gather(table, lane):
    return lax.gather(
        table, lane[..., None], WITHIN, (1, 1), mode=lax.GatherScatterMode.PROMISE_IN_BOUNDS
    )


def pick_kernel(
    order, feats_hbm, ids_hbm, counts_hbm, self_hbm, neigh_hbm, out_ref,
    feats_ref, ids_ref, counts_ref, self_ref, neigh_ref, wide, table, sums, arrived,
):
    copies = [
        pltpu.make_async_copy(source, target, arrived.at[i])
        for i, (source, target) in enumerate(
            (
                (feats_hbm, feats_ref),
                (ids_hbm, ids_ref),
                (counts_hbm, counts_ref),
                (self_hbm, self_ref),
                (neigh_hbm, neigh_ref),
            )
        )
    ]
    for copy in copies:
        copy.start()
    rows, nodes = feats_ref.shape
    fan = ids_ref.shape[0]
    blocks = nodes // LANES
    copies[0].wait()
    values = feats_ref[...].astype(jnp.float32)
    wide[0:rows, :] = values
    wide[rows : 2 * rows, :] = values
    table[...] = jnp.concatenate([wide[...]] * 2, axis=0).astype(jnp.bfloat16)
    for copy in copies[1:]:
        copy.wait()
    row = lax.broadcasted_iota(jnp.int32, (4 * rows, LANES), 0)
    upper = lax.broadcasted_iota(jnp.int32, (2 * rows, LANES), 0) < rows

    def four_blocks(quad, carry):
        start = pl.multiple_of(quad * 4 * LANES, 4 * LANES)

        def spread(ref, k):
            parts = [
                jnp.broadcast_to(ref[k : k + 1, pl.ds(start + i * LANES, LANES)], row.shape)
                for i in range(4)
            ]
            return jnp.where(
                row < 2 * rows,
                jnp.where(row < rows, parts[0], parts[1]),
                jnp.where(row < 3 * rows, parts[2], parts[3]),
            )

        counts = spread(counts_ref, 0)
        total = jnp.zeros(row.shape, jnp.float32)
        for k in range(fan):
            ids = spread(ids_ref, k)
            lane = jnp.bitwise_and(ids, LANES - 1).astype(jnp.int16)
            block = lax.shift_right_logical(ids, 7).astype(jnp.int16)
            level = [
                lane_gather(table[:, j * LANES : (j + 1) * LANES], lane) for j in range(blocks)
            ]
            bit = 1
            while len(level) > 1:
                odd = jnp.bitwise_and(block, jnp.int16(bit)) != 0
                level = [
                    jnp.where(odd, level[i + 1], level[i]) for i in range(0, len(level), 2)
                ]
                bit *= 2
            total = total + jnp.where(counts > k, level[0].astype(jnp.float32), 0.0)
        mean = total / counts.astype(jnp.float32)
        for i in range(4):
            half = mean[(i // 2) * 2 * rows : (i // 2 + 1) * 2 * rows]
            if i % 2 == 0:
                half = pltpu.roll(half, rows, axis=0)
            to = pl.multiple_of(start + (i + 1) * LANES, LANES)
            sums[:, pl.ds(to, LANES)] = jnp.where(
                upper, wide[:, pl.ds(start + i * LANES, LANES)], half
            )
        return carry

    lax.fori_loop(0, blocks // 4, four_blocks, 0, unroll=True)
    sums[:, 0:LANES] = sums[:, blocks * LANES : (blocks + 1) * LANES]
    sums[:, (blocks + 1) * LANES :] = sums[:, LANES : 2 * LANES]
    weights = jnp.concatenate(
        [self_ref[...].astype(jnp.float32), neigh_ref[...].astype(jnp.float32)], axis=0
    ).astype(jnp.bfloat16)
    for first in range(0, blocks, 2):
        span = sums[:, first * LANES : (first + 4) * LANES].astype(jnp.bfloat16)
        for block in (first, first + 1):
            to = order.index(block)
            out_ref[to, :, 0 : 4 * LANES] = span
            out_ref[to, :, 4 * LANES :] = weights


def gelu_parts(value):
    square = value * value
    bent = jnp.tanh(INNER * (value + CUBIC * (value * square)))
    half = 0.5 * (1.0 + bent)
    slope = half + 0.5 * value * (1.0 - bent * bent) * (INNER * (1.0 + 3.0 * CUBIC * square))
    return value * half, slope


def layers_kernel(
    core_ref, got_ref, own_meta_ref, other_meta_ref, counts_ref, bias_ref, self_ref, neigh_ref,
    own_cot_ref, other_cot_ref, hidden_ref, parts_ref,
):
    node_rows, hid = own_cot_ref.shape
    span = 4 * node_rows
    fan = own_meta_ref.shape[0]
    over_rows = (((0,), (0,)), ((), ()))
    is_first = core_ref[0] == 0
    got = got_ref[...]
    pre_one = lax.dot_general(
        got[:, :span], got[:, span:], over_rows, preferred_element_type=jnp.float32
    )
    hidden = gelu_parts(pre_one + bias_ref[0:1, :])[0].astype(jnp.bfloat16)
    own = hidden[node_rows : 3 * node_rows]
    own_meta, other_meta = own_meta_ref[...], other_meta_ref[...]
    number = lax.broadcasted_iota(jnp.int32, (span, node_rows), 0).astype(jnp.int16)
    one, zero = jnp.ones((), jnp.bfloat16), jnp.zeros((), jnp.bfloat16)
    often = []
    for meta in (
        jnp.where(is_first, own_meta, other_meta),
        jnp.where(is_first, other_meta, own_meta),
    ):
        total = jnp.zeros((span, node_rows), jnp.bfloat16)
        for k in range(fan):
            ids = jnp.broadcast_to(meta[k : k + 1, :], (span, node_rows)).astype(jnp.int16)
            total = total + jnp.where(ids == number, one, zero)
        often.append(total)
    summed = lax.dot_general(
        jnp.concatenate(often, axis=1), hidden, over_rows, preferred_element_type=jnp.float32
    )
    agg = (summed / counts_ref[...].astype(jnp.float32)).astype(jnp.bfloat16)
    pre_two = jnp.dot(own, self_ref[...], preferred_element_type=jnp.float32)
    pre_two = pre_two + jnp.dot(agg, neigh_ref[...], preferred_element_type=jnp.float32)
    value, slope = gelu_parts(pre_two + bias_ref[1:2, :])
    hidden_ref[...] = jnp.where(is_first, value[:node_rows], value[node_rows:]).astype(jnp.bfloat16)
    own_cot = own_cot_ref[...].astype(jnp.float32)
    other_cot = other_cot_ref[...].astype(jnp.float32)
    cot = jnp.concatenate(
        [jnp.where(is_first, own_cot, other_cot), jnp.where(is_first, other_cot, own_cot)], axis=0
    )
    delta = (cot * slope).astype(jnp.bfloat16)
    rows = jnp.where(is_first, own, agg)
    grads = lax.dot_general(rows, delta, over_rows, preferred_element_type=jnp.float32)
    bias = jnp.sum(delta.astype(jnp.float32), axis=0, keepdims=True)
    row = lax.broadcasted_iota(jnp.int32, (8, LANES), 0)
    halves = jnp.where(
        row == 0,
        jnp.broadcast_to(bias[:, :LANES], row.shape),
        jnp.where(row == 1, jnp.broadcast_to(bias[:, LANES:], row.shape), 0.0),
    )
    for part in range(parts_ref.shape[0]):
        parts_ref[part, 0:8, :] = grads[part * 8 : part * 8 + 8, :LANES]
        parts_ref[part, 8:16, :] = grads[part * 8 : part * 8 + 8, LANES:]
        parts_ref[part, 16:24, :] = halves


def repeat_kernel(part_ref, out_ref):
    part = jnp.concatenate([part_ref[0:8, :], part_ref[8:16, :]], axis=1).astype(jnp.bfloat16)
    for to in range(out_ref.shape[0]):
        out_ref[to] = part


def widen_kernel(got_ref, self_ref, neigh_ref):
    parts, _, rows, _ = got_ref.shape
    for part in range(parts):
        self_ref[part * rows : (part + 1) * rows, :] = got_ref[part, 0].astype(jnp.float32)
        neigh_ref[part * rows : (part + 1) * rows, :] = got_ref[part, 1].astype(jnp.float32)


def from_member(first, size):
    return [(first + i) % size for i in range(size)]


def local(
    features,
    neighbours_one,
    counts_one,
    neighbours_two,
    counts_two,
    self_one,
    neigh_one,
    bias_one,
    self_two,
    neigh_two,
    bias_two,
    cotangent,
):
    rows, batch_nodes = features.shape
    pairs, chips, cores = lax.axis_size("pair"), lax.axis_size("chip"), lax.axis_size("core")
    others = lax.axis_size("apart")
    groups = chips * cores
    node_rows = batch_nodes // groups
    hid = self_one.shape[1]
    span = 4 * node_rows
    params = pltpu.CompilerParams(vmem_limit_bytes=VMEM_BYTES)
    group = pairs * chips
    everyone = group * cores
    first_chip = chips // 2 + chips // 8
    first_part = group - chips + first_chip
    feat_order = from_member(first_chip * cores, groups)
    part_order = from_member(first_part, group)
    every_order = from_member(first_part * cores, everyone)
    apart_order = from_member(others // 2, others)
    chunks = pl.pallas_call(
        functools.partial(pick_kernel, feat_order),
        out_shape=jax.ShapeDtypeStruct((groups, 2 * rows, span + hid), jnp.bfloat16),
        in_specs=[pl.BlockSpec(memory_space=pltpu.HBM)] * 5,
        scratch_shapes=[
            pltpu.VMEM(features.shape, features.dtype),
            pltpu.VMEM(neighbours_one.shape[::-1], jnp.int32),
            pltpu.VMEM((1, batch_nodes), jnp.int32),
            pltpu.VMEM(self_one.shape, self_one.dtype),
            pltpu.VMEM(neigh_one.shape, neigh_one.dtype),
            pltpu.VMEM((2 * rows, batch_nodes), jnp.float32),
            pltpu.VMEM((4 * rows, batch_nodes), jnp.bfloat16),
            pltpu.VMEM((2 * rows, batch_nodes + 2 * node_rows), jnp.float32),
            pltpu.SemaphoreType.DMA((5,)),
        ],
        compiler_params=pltpu.CompilerParams(vmem_limit_bytes=PICK_VMEM_BYTES),
        name="pick",
    )(features, neighbours_one.T, counts_one[None, :], self_one, neigh_one)
    got = lax.all_to_all(
        chunks, ("chip", "core"), 0, 0, tiled=True, axis_index_groups=[feat_order]
    )

    swap = [(0, 1), (1, 0)]
    core = lax.axis_index("core")
    first_node = (lax.axis_index("chip") * cores - 1) * node_rows
    meta = jnp.concatenate([neighbours_two.T, counts_two[None, :]], axis=0)
    other_meta = lax.ppermute(meta, "core", swap)
    other_cot = lax.ppermute(cotangent, "core", swap)

    def numbers(kept):
        live = jnp.arange(kept.shape[0] - 1, dtype=jnp.int32)[:, None] < kept[-1:]
        return jnp.where(live, kept[:-1] - first_node, -1)

    counts = jnp.where(
        core == 0,
        jnp.concatenate([counts_two, other_meta[-1]]),
        jnp.concatenate([other_meta[-1], counts_two]),
    )
    hidden_two, parts = pl.pallas_call(
        layers_kernel,
        out_shape=(
            jax.ShapeDtypeStruct((node_rows, hid), jnp.bfloat16),
            jax.ShapeDtypeStruct((group, 24, LANES), jnp.float32),
        ),
        in_specs=[pl.BlockSpec(memory_space=pltpu.SMEM)]
        + [pl.BlockSpec(memory_space=pltpu.VMEM)] * 9,
        compiler_params=params,
        name="layers",
    )(
        core[None],
        got.reshape(groups * 2 * rows, span + hid),
        numbers(meta),
        numbers(other_meta),
        counts[:, None],
        jnp.stack([bias_one, bias_two]),
        self_two,
        neigh_two,
        cotangent,
        other_cot,
    )
    inner = lax.all_to_all(
        parts, ("pair", "chip"), 0, 0, tiled=True, axis_index_groups=[part_order]
    ).sum(axis=0)
    inner = inner[:18].reshape(9, 2, LANES)
    spread = jnp.broadcast_to(inner[None], (others,) + inner.shape)
    total = lax.all_to_all(
        spread, "apart", 0, 0, tiled=True, axis_index_groups=[apart_order]
    ).sum(axis=0)
    total = total.reshape(18, LANES) * (1.0 / (batch_nodes * pairs * others))
    spread = pl.pallas_call(
        repeat_kernel,
        out_shape=jax.ShapeDtypeStruct((everyone, hid // group, hid), jnp.bfloat16),
        compiler_params=params,
        name="repeat",
    )(total)
    whole = lax.all_to_all(
        spread, ("pair", "chip", "core"), 0, 0, tiled=True, axis_index_groups=[every_order]
    )
    grad_self, grad_neigh = pl.pallas_call(
        widen_kernel,
        out_shape=(jax.ShapeDtypeStruct((hid, hid), jnp.float32),) * 2,
        compiler_params=params,
        name="widen",
    )(whole.reshape(group, cores, hid // group, hid))
    return hidden_two, grad_self, grad_neigh, total[16:].reshape(hid)


def solution(mesh):
    replicas, groups = mesh.devices.shape
    split = Mesh(
        mesh.devices.reshape(replicas // 2, 2, groups // 2, 2), ("apart", "pair", "chip", "core")
    )
    dp = ("apart", "pair")
    feat = ("chip", "core")
    every = dp + feat
    return jax.shard_map(
        local,
        mesh=split,
        in_specs=(
            P(feat, dp),
            P(dp, None),
            P(dp),
            P(every, None),
            P(every),
            P(feat, None),
            P(feat, None),
            P(),
            P(),
            P(),
            P(),
            P(every, None),
        ),
        out_specs=(P(every, None), P(), P(), P()),
        check_vma=False,
    )
```

```python
import functools
import math

import jax
import jax.numpy as jnp
from jax import lax
from jax.experimental import pallas as pl
from jax.experimental.pallas import tpu as pltpu
from jax.sharding import Mesh
from jax.sharding import PartitionSpec as P

LANES = 128
INNER = math.sqrt(2.0 / math.pi)
CUBIC = 0.044715
VMEM_BYTES = 48 * 1024 * 1024
PICK_VMEM_BYTES = 57_000_000


WITHIN = lax.GatherDimensionNumbers(
    offset_dims=(),
    collapsed_slice_dims=(1,),
    start_index_map=(1,),
    operand_batching_dims=(0,),
    start_indices_batching_dims=(0,),
)


def lane_gather(table, lane):
    return lax.gather(
        table, lane[..., None], WITHIN, (1, 1), mode=lax.GatherScatterMode.PROMISE_IN_BOUNDS
    )


def pick_kernel(
    order, feats_hbm, ids_hbm, counts_hbm, self_hbm, neigh_hbm, out_ref, zeros_ref,
    feats_ref, ids_ref, counts_ref, self_ref, neigh_ref, wide, table, sums, arrived,
):
    copies = [
        pltpu.make_async_copy(source, target, arrived.at[i])
        for i, (source, target) in enumerate(
            (
                (feats_hbm, feats_ref),
                (ids_hbm, ids_ref),
                (counts_hbm, counts_ref),
                (self_hbm, self_ref),
                (neigh_hbm, neigh_ref),
            )
        )
    ]
    for copy in copies:
        copy.start()
    zeros_ref[...] = jnp.zeros_like(zeros_ref)
    rows, nodes = feats_ref.shape
    fan = ids_ref.shape[0]
    blocks = nodes // LANES
    copies[0].wait()
    values = feats_ref[...].astype(jnp.float32)
    wide[0:rows, :] = values
    wide[rows : 2 * rows, :] = values
    table[...] = jnp.concatenate([wide[...]] * 2, axis=0).astype(jnp.bfloat16)
    for copy in copies[1:]:
        copy.wait()
    row = lax.broadcasted_iota(jnp.int32, (4 * rows, LANES), 0)
    upper = lax.broadcasted_iota(jnp.int32, (2 * rows, LANES), 0) < rows

    def four_blocks(quad, carry):
        start = pl.multiple_of(quad * 4 * LANES, 4 * LANES)

        def spread(ref, k):
            parts = [
                jnp.broadcast_to(ref[k : k + 1, pl.ds(start + i * LANES, LANES)], row.shape)
                for i in range(4)
            ]
            return jnp.where(
                row < 2 * rows,
                jnp.where(row < rows, parts[0], parts[1]),
                jnp.where(row < 3 * rows, parts[2], parts[3]),
            )

        counts = spread(counts_ref, 0)
        total = jnp.zeros(row.shape, jnp.float32)
        for k in range(fan):
            ids = spread(ids_ref, k)
            lane = jnp.bitwise_and(ids, LANES - 1).astype(jnp.int16)
            block = lax.shift_right_logical(ids, 7).astype(jnp.int16)
            level = [
                lane_gather(table[:, j * LANES : (j + 1) * LANES], lane) for j in range(blocks)
            ]
            bit = 1
            while len(level) > 1:
                odd = jnp.bitwise_and(block, jnp.int16(bit)) != 0
                level = [
                    jnp.where(odd, level[i + 1], level[i]) for i in range(0, len(level), 2)
                ]
                bit *= 2
            total = total + jnp.where(counts > k, level[0].astype(jnp.float32), 0.0)
        mean = total / counts.astype(jnp.float32)
        for i in range(4):
            half = mean[(i // 2) * 2 * rows : (i // 2 + 1) * 2 * rows]
            if i % 2 == 0:
                half = pltpu.roll(half, rows, axis=0)
            to = pl.multiple_of(start + (i + 1) * LANES, LANES)
            sums[:, pl.ds(to, LANES)] = jnp.where(
                upper, wide[:, pl.ds(start + i * LANES, LANES)], half
            )
        return carry

    lax.fori_loop(0, blocks // 4, four_blocks, 0, unroll=True)
    sums[:, 0:LANES] = sums[:, blocks * LANES : (blocks + 1) * LANES]
    sums[:, (blocks + 1) * LANES :] = sums[:, LANES : 2 * LANES]
    weights = jnp.concatenate(
        [self_ref[...].astype(jnp.float32), neigh_ref[...].astype(jnp.float32)], axis=0
    ).astype(jnp.bfloat16)
    for first in range(0, blocks, 2):
        span = sums[:, first * LANES : (first + 4) * LANES].astype(jnp.bfloat16)
        for block in (first, first + 1):
            to = order.index(block)
            out_ref[to, :, 0 : 4 * LANES] = span
            out_ref[to, :, 4 * LANES :] = weights


def gelu_parts(value):
    square = value * value
    bent = jnp.tanh(INNER * (value + CUBIC * (value * square)))
    half = 0.5 * (1.0 + bent)
    slope = half + 0.5 * value * (1.0 - bent * bent) * (INNER * (1.0 + 3.0 * CUBIC * square))
    return value * half, slope


def layers_kernel(
    core_ref, got_ref, own_meta_ref, other_meta_ref, counts_ref, bias_ref, self_ref, neigh_ref,
    own_cot_ref, other_cot_ref, hidden_ref, parts_ref,
):
    node_rows, hid = own_cot_ref.shape
    span = 4 * node_rows
    fan = own_meta_ref.shape[0]
    over_rows = (((0,), (0,)), ((), ()))
    is_first = core_ref[0] == 0
    got = got_ref[...]
    pre_one = lax.dot_general(
        got[:, :span], got[:, span:], over_rows, preferred_element_type=jnp.float32
    )
    hidden = gelu_parts(pre_one + bias_ref[0:1, :])[0].astype(jnp.bfloat16)
    own = hidden[node_rows : 3 * node_rows]
    own_meta, other_meta = own_meta_ref[...], other_meta_ref[...]
    number = lax.broadcasted_iota(jnp.int32, (span, node_rows), 0).astype(jnp.int16)
    one, zero = jnp.ones((), jnp.bfloat16), jnp.zeros((), jnp.bfloat16)
    often = []
    for meta in (
        jnp.where(is_first, own_meta, other_meta),
        jnp.where(is_first, other_meta, own_meta),
    ):
        total = jnp.zeros((span, node_rows), jnp.bfloat16)
        for k in range(fan):
            ids = jnp.broadcast_to(meta[k : k + 1, :], (span, node_rows)).astype(jnp.int16)
            total = total + jnp.where(ids == number, one, zero)
        often.append(total)
    summed = lax.dot_general(
        jnp.concatenate(often, axis=1), hidden, over_rows, preferred_element_type=jnp.float32
    )
    agg = (summed / counts_ref[...].astype(jnp.float32)).astype(jnp.bfloat16)
    pre_two = jnp.dot(own, self_ref[...], preferred_element_type=jnp.float32)
    pre_two = pre_two + jnp.dot(agg, neigh_ref[...], preferred_element_type=jnp.float32)
    value, slope = gelu_parts(pre_two + bias_ref[1:2, :])
    hidden_ref[...] = jnp.where(is_first, value[:node_rows], value[node_rows:]).astype(jnp.bfloat16)
    own_cot = own_cot_ref[...].astype(jnp.float32)
    other_cot = other_cot_ref[...].astype(jnp.float32)
    cot = jnp.concatenate(
        [jnp.where(is_first, own_cot, other_cot), jnp.where(is_first, other_cot, own_cot)], axis=0
    )
    delta = (cot * slope).astype(jnp.bfloat16)
    rows = jnp.where(is_first, own, agg)
    grads = lax.dot_general(rows, delta, over_rows, preferred_element_type=jnp.float32)
    bias = jnp.sum(delta.astype(jnp.float32), axis=0, keepdims=True)
    for half in range(2):
        columns = slice(half * LANES, (half + 1) * LANES)
        for part in range(parts_ref.shape[0]):
            parts_ref[part, 4 * half : 4 * half + 4] = grads[
                part * 8 : part * 8 + 8, columns
            ].reshape(4, 2, LANES)
            parts_ref[part, 8, half : half + 1, :] = bias[:, columns]


def repeat_kernel(part_ref, out_ref):
    part = jnp.concatenate([part_ref[0:8, :], part_ref[8:16, :]], axis=1).astype(jnp.bfloat16)
    for to in range(out_ref.shape[0]):
        out_ref[to] = part


def widen_kernel(got_ref, self_ref, neigh_ref):
    parts, _, rows, _ = got_ref.shape
    for part in range(parts):
        self_ref[part * rows : (part + 1) * rows, :] = got_ref[part, 0].astype(jnp.float32)
        neigh_ref[part * rows : (part + 1) * rows, :] = got_ref[part, 1].astype(jnp.float32)


def from_member(first, size):
    return [(first + i) % size for i in range(size)]


def local(
    features,
    neighbours_one,
    counts_one,
    neighbours_two,
    counts_two,
    self_one,
    neigh_one,
    bias_one,
    self_two,
    neigh_two,
    bias_two,
    cotangent,
):
    rows, batch_nodes = features.shape
    pairs, chips, cores = lax.axis_size("pair"), lax.axis_size("chip"), lax.axis_size("core")
    others = lax.axis_size("apart")
    groups = chips * cores
    node_rows = batch_nodes // groups
    hid = self_one.shape[1]
    span = 4 * node_rows
    params = pltpu.CompilerParams(vmem_limit_bytes=VMEM_BYTES)
    group = pairs * chips
    everyone = group * cores
    first_chip = chips // 2 + chips // 8
    first_part = group - chips + first_chip
    feat_order = from_member(first_chip * cores, groups)
    part_order = from_member(first_part, group)
    every_order = from_member(first_part * cores, everyone)
    apart_order = from_member(others // 2, others)
    chunks, zeros = pl.pallas_call(
        functools.partial(pick_kernel, feat_order),
        out_shape=(
            jax.ShapeDtypeStruct((groups, 2 * rows, span + hid), jnp.bfloat16),
            jax.ShapeDtypeStruct((1, hid), jnp.int32),
        ),
        in_specs=[pl.BlockSpec(memory_space=pltpu.HBM)] * 5,
        scratch_shapes=[
            pltpu.VMEM(features.shape, features.dtype),
            pltpu.VMEM(neighbours_one.shape[::-1], jnp.int32),
            pltpu.VMEM((1, batch_nodes), jnp.int32),
            pltpu.VMEM(self_one.shape, self_one.dtype),
            pltpu.VMEM(neigh_one.shape, neigh_one.dtype),
            pltpu.VMEM((2 * rows, batch_nodes), jnp.float32),
            pltpu.VMEM((4 * rows, batch_nodes), jnp.bfloat16),
            pltpu.VMEM((2 * rows, batch_nodes + 2 * node_rows), jnp.float32),
            pltpu.SemaphoreType.DMA((5,)),
        ],
        compiler_params=pltpu.CompilerParams(vmem_limit_bytes=PICK_VMEM_BYTES),
        name="pick",
    )(features, neighbours_one.T, counts_one[None, :], self_one, neigh_one)
    got = lax.all_to_all(
        chunks, ("chip", "core"), 0, 0, tiled=True, axis_index_groups=[feat_order]
    )

    swap = [(0, 1), (1, 0)]
    core = lax.axis_index("core")
    first_node = (lax.axis_index("chip") * cores - 1) * node_rows
    meta = jnp.concatenate([neighbours_two.T, counts_two[None, :]], axis=0)
    meta = meta + zeros[:, : meta.shape[1]]
    other_meta = lax.ppermute(meta, "core", swap)
    other_cot = lax.ppermute(jnp.where(zeros == 0, cotangent, 0), "core", swap)

    def numbers(kept):
        live = jnp.arange(kept.shape[0] - 1, dtype=jnp.int32)[:, None] < kept[-1:]
        return jnp.where(live, kept[:-1] - first_node, -1)

    counts = jnp.where(
        core == 0,
        jnp.concatenate([counts_two, other_meta[-1]]),
        jnp.concatenate([other_meta[-1], counts_two]),
    )
    hidden_two, parts = pl.pallas_call(
        layers_kernel,
        out_shape=(
            jax.ShapeDtypeStruct((node_rows, hid), jnp.bfloat16),
            jax.ShapeDtypeStruct((group, 9, 2, LANES), jnp.float32),
        ),
        in_specs=[pl.BlockSpec(memory_space=pltpu.SMEM)]
        + [pl.BlockSpec(memory_space=pltpu.VMEM)] * 9,
        compiler_params=params,
        name="layers",
    )(
        core[None],
        got.reshape(groups * 2 * rows, span + hid),
        numbers(meta),
        numbers(other_meta),
        counts[:, None],
        jnp.stack([bias_one, bias_two]),
        self_two,
        neigh_two,
        cotangent,
        other_cot,
    )
    inner = lax.all_to_all(
        parts, ("pair", "chip"), 0, 0, tiled=True, axis_index_groups=[part_order]
    ).sum(axis=0)
    spread = jnp.broadcast_to(inner[None], (others,) + inner.shape)
    total = lax.all_to_all(
        spread, "apart", 0, 0, tiled=True, axis_index_groups=[apart_order]
    ).sum(axis=0)
    total = total.reshape(18, LANES) * (1.0 / (batch_nodes * pairs * others))
    spread = pl.pallas_call(
        repeat_kernel,
        out_shape=jax.ShapeDtypeStruct((everyone, hid // group, hid), jnp.bfloat16),
        compiler_params=params,
        name="repeat",
    )(total)
    whole = lax.all_to_all(
        spread, ("pair", "chip", "core"), 0, 0, tiled=True, axis_index_groups=[every_order]
    )
    grad_self, grad_neigh = pl.pallas_call(
        widen_kernel,
        out_shape=(jax.ShapeDtypeStruct((hid, hid), jnp.float32),) * 2,
        compiler_params=params,
        name="widen",
    )(whole.reshape(group, cores, hid // group, hid))
    return hidden_two, grad_self, grad_neigh, total[16:].reshape(hid)


def solution(mesh):
    replicas, groups = mesh.devices.shape
    split = Mesh(
        mesh.devices.reshape(replicas // 2, 2, groups // 2, 2), ("apart", "pair", "chip", "core")
    )
    dp = ("apart", "pair")
    feat = ("chip", "core")
    every = dp + feat
    return jax.shard_map(
        local,
        mesh=split,
        in_specs=(
            P(feat, dp),
            P(dp, None),
            P(dp),
            P(every, None),
            P(every),
            P(feat, None),
            P(feat, None),
            P(),
            P(),
            P(),
            P(),
            P(every, None),
        ),
        out_specs=(P(every, None), P(), P(), P()),
        check_vma=False,
    )
```

```python
import functools
import math

import jax
import jax.numpy as jnp
from jax import lax
from jax.experimental import pallas as pl
from jax.experimental.pallas import tpu as pltpu
from jax.sharding import Mesh
from jax.sharding import PartitionSpec as P

LANES = 128
DEAD = -64
INNER = math.sqrt(2.0 / math.pi)
CUBIC = 0.044715
VMEM_BYTES = 48 * 1024 * 1024
PICK_VMEM_BYTES = 57_000_000


WITHIN = lax.GatherDimensionNumbers(
    offset_dims=(),
    collapsed_slice_dims=(1,),
    start_index_map=(1,),
    operand_batching_dims=(0,),
    start_indices_batching_dims=(0,),
)


def lane_gather(table, lane):
    return lax.gather(
        table, lane[..., None], WITHIN, (1, 1), mode=lax.GatherScatterMode.PROMISE_IN_BOUNDS
    )


def pick_kernel(
    order, feats_hbm, ids_hbm, counts_hbm, self_hbm, neigh_hbm, ids_two_hbm, counts_two_hbm,
    cot_hbm, bias_one_hbm, bias_two_hbm, out_ref, send_ref, biases_ref,
    feats_ref, ids_ref, counts_ref, self_ref, neigh_ref, ids_two_ref, counts_two_ref, cot_ref,
    bias_one_ref, bias_two_ref, wide, table, sums, lists, arrived,
):
    copies = [
        pltpu.make_async_copy(source, target, arrived.at[i])
        for i, (source, target) in enumerate(
            (
                (feats_hbm, feats_ref),
                (ids_hbm, ids_ref),
                (counts_hbm, counts_ref),
                (self_hbm, self_ref),
                (neigh_hbm, neigh_ref),
                (ids_two_hbm, ids_two_ref),
                (counts_two_hbm, counts_two_ref),
                (cot_hbm, cot_ref),
                (bias_one_hbm, bias_one_ref),
                (bias_two_hbm, bias_two_ref),
            )
        )
    ]
    for copy in copies:
        copy.start()
    rows, nodes = feats_ref.shape
    fan = ids_ref.shape[0]
    blocks = nodes // LANES
    copies[0].wait()
    values = feats_ref[...].astype(jnp.float32)
    wide[0:rows, :] = values
    wide[rows : 2 * rows, :] = values
    table[...] = jnp.concatenate([wide[...]] * 2, axis=0).astype(jnp.bfloat16)
    for copy in copies[1:]:
        copy.wait()
    row = lax.broadcasted_iota(jnp.int32, (4 * rows, LANES), 0)
    upper = lax.broadcasted_iota(jnp.int32, (2 * rows, LANES), 0) < rows

    def four_blocks(quad, carry):
        start = pl.multiple_of(quad * 4 * LANES, 4 * LANES)

        def spread(ref, k):
            parts = [
                jnp.broadcast_to(ref[k : k + 1, pl.ds(start + i * LANES, LANES)], row.shape)
                for i in range(4)
            ]
            return jnp.where(
                row < 2 * rows,
                jnp.where(row < rows, parts[0], parts[1]),
                jnp.where(row < 3 * rows, parts[2], parts[3]),
            )

        counts = spread(counts_ref, 0)
        total = jnp.zeros(row.shape, jnp.float32)
        for k in range(fan):
            ids = spread(ids_ref, k)
            lane = jnp.bitwise_and(ids, LANES - 1).astype(jnp.int16)
            block = lax.shift_right_logical(ids, 7).astype(jnp.int16)
            level = [
                lane_gather(table[:, j * LANES : (j + 1) * LANES], lane) for j in range(blocks)
            ]
            bit = 1
            while len(level) > 1:
                odd = jnp.bitwise_and(block, jnp.int16(bit)) != 0
                level = [
                    jnp.where(odd, level[i + 1], level[i]) for i in range(0, len(level), 2)
                ]
                bit *= 2
            total = total + jnp.where(counts > k, level[0].astype(jnp.float32), 0.0)
        mean = total / counts.astype(jnp.float32)
        for i in range(4):
            half = mean[(i // 2) * 2 * rows : (i // 2 + 1) * 2 * rows]
            if i % 2 == 0:
                half = pltpu.roll(half, rows, axis=0)
            to = pl.multiple_of(start + (i + 1) * LANES, LANES)
            sums[:, pl.ds(to, LANES)] = jnp.where(
                upper, wide[:, pl.ds(start + i * LANES, LANES)], half
            )
        return carry

    lax.fori_loop(0, blocks // 4, four_blocks, 0, unroll=True)
    sums[:, 0:LANES] = sums[:, blocks * LANES : (blocks + 1) * LANES]
    sums[:, (blocks + 1) * LANES :] = sums[:, LANES : 2 * LANES]
    node_rows = cot_ref.shape[0]
    fan_two = ids_two_ref.shape[0]
    lists[...] = jnp.zeros_like(lists)
    lists[0:fan_two, :] = ids_two_ref[...]
    row = lax.broadcasted_iota(jnp.int32, lists.shape, 0)
    counts_two = jnp.broadcast_to(counts_two_ref[...], lists.shape)
    place = jnp.bitwise_and(lists[...], LANES - 1)
    block = jnp.where(row < counts_two, lax.shift_right_logical(lists[...], 7), DEAD)
    place = jnp.where(row == fan_two, counts_two, place)
    send_ref[0:node_rows, :] = cot_ref[...]
    send_ref[node_rows:, 0:LANES] = place.astype(jnp.float32).astype(jnp.bfloat16)
    send_ref[node_rows:, LANES:] = block.astype(jnp.float32).astype(jnp.bfloat16)
    biases_ref[0:1, :] = bias_one_ref[...]
    biases_ref[1:2, :] = bias_two_ref[...]
    weights = jnp.concatenate(
        [self_ref[...].astype(jnp.float32), neigh_ref[...].astype(jnp.float32)], axis=0
    ).astype(jnp.bfloat16)
    for first in range(0, blocks, 2):
        span = sums[:, first * LANES : (first + 4) * LANES].astype(jnp.bfloat16)
        for block in (first, first + 1):
            to = order.index(block)
            out_ref[to, :, 0 : 4 * LANES] = span
            out_ref[to, :, 4 * LANES :] = weights


def gelu_parts(value):
    square = value * value
    bent = jnp.tanh(INNER * (value + CUBIC * (value * square)))
    half = 0.5 * (1.0 + bent)
    slope = half + 0.5 * value * (1.0 - bent * bent) * (INNER * (1.0 + 3.0 * CUBIC * square))
    return value * half, slope


def layers_kernel(
    fan, place_ref, got_ref, own_ref, other_ref, bias_ref, self_ref, neigh_ref, hidden_ref, parts_ref,
):
    node_rows, hid = hidden_ref.shape
    span = 4 * node_rows
    over_rows = (((0,), (0,)), ((), ()))
    is_first, first_block = place_ref[0] == 0, place_ref[1]
    got = got_ref[...]
    pre_one = lax.dot_general(
        got[:, :span], got[:, span:], over_rows, preferred_element_type=jnp.float32
    )
    hidden = gelu_parts(pre_one + bias_ref[0:1, :])[0].astype(jnp.bfloat16)
    own = hidden[node_rows : 3 * node_rows]

    def lists_of(ref):
        kept = ref[node_rows:, :].astype(jnp.float32)
        place = kept[:, :LANES]
        numbers = (kept[:, LANES:].astype(jnp.int32) - first_block) * LANES + place.astype(jnp.int32)
        return numbers, place

    def in_order(own, other):
        return jnp.where(is_first, own, other), jnp.where(is_first, other, own)

    own_lists, other_lists = lists_of(own_ref), lists_of(other_ref)
    number = lax.broadcasted_iota(jnp.int32, (span, node_rows), 0).astype(jnp.int16)
    one, zero = jnp.ones((), jnp.bfloat16), jnp.zeros((), jnp.bfloat16)
    often = []
    for numbers in in_order(own_lists[0], other_lists[0]):
        total = jnp.zeros((span, node_rows), jnp.bfloat16)
        for k in range(fan):
            ids = jnp.broadcast_to(numbers[k : k + 1, :], (span, node_rows)).astype(jnp.int16)
            total = total + jnp.where(ids == number, one, zero)
        often.append(total)
    counts = jnp.concatenate(
        [
            jnp.broadcast_to(places[fan : fan + 1, :], (LANES, LANES)).T
            for places in in_order(own_lists[1], other_lists[1])
        ],
        axis=0,
    )
    summed = lax.dot_general(
        jnp.concatenate(often, axis=1), hidden, over_rows, preferred_element_type=jnp.float32
    )
    agg = (summed / jnp.concatenate([counts] * (hid // LANES), axis=1)).astype(jnp.bfloat16)
    pre_two = jnp.dot(own, self_ref[...], preferred_element_type=jnp.float32)
    pre_two = pre_two + jnp.dot(agg, neigh_ref[...], preferred_element_type=jnp.float32)
    value, slope = gelu_parts(pre_two + bias_ref[1:2, :])
    hidden_ref[...] = jnp.where(is_first, value[:node_rows], value[node_rows:]).astype(jnp.bfloat16)
    cot = jnp.concatenate(
        in_order(
            own_ref[0:node_rows, :].astype(jnp.float32), other_ref[0:node_rows, :].astype(jnp.float32)
        ),
        axis=0,
    )
    delta = (cot * slope).astype(jnp.bfloat16)
    rows = jnp.where(is_first, own, agg)
    grads = lax.dot_general(rows, delta, over_rows, preferred_element_type=jnp.float32)
    bias = jnp.sum(delta.astype(jnp.float32), axis=0, keepdims=True)
    for half in range(2):
        columns = slice(half * LANES, (half + 1) * LANES)
        for part in range(parts_ref.shape[0]):
            parts_ref[part, 4 * half : 4 * half + 4] = grads[
                part * 8 : part * 8 + 8, columns
            ].reshape(4, 2, LANES)
            parts_ref[part, 8, half : half + 1, :] = bias[:, columns]


def repeat_kernel(part_ref, out_ref):
    part = jnp.concatenate([part_ref[0:8, :], part_ref[8:16, :]], axis=1).astype(jnp.bfloat16)
    for to in range(out_ref.shape[0]):
        out_ref[to] = part


def widen_kernel(got_ref, self_ref, neigh_ref):
    parts, _, rows, _ = got_ref.shape
    for part in range(parts):
        self_ref[part * rows : (part + 1) * rows, :] = got_ref[part, 0].astype(jnp.float32)
        neigh_ref[part * rows : (part + 1) * rows, :] = got_ref[part, 1].astype(jnp.float32)


def from_member(first, size):
    return [(first + i) % size for i in range(size)]


def local(
    features,
    neighbours_one,
    counts_one,
    neighbours_two,
    counts_two,
    self_one,
    neigh_one,
    bias_one,
    self_two,
    neigh_two,
    bias_two,
    cotangent,
):
    rows, batch_nodes = features.shape
    pairs, chips, cores = lax.axis_size("pair"), lax.axis_size("chip"), lax.axis_size("core")
    others = lax.axis_size("apart")
    groups = chips * cores
    node_rows = batch_nodes // groups
    hid = self_one.shape[1]
    span = 4 * node_rows
    params = pltpu.CompilerParams(vmem_limit_bytes=VMEM_BYTES)
    group = pairs * chips
    everyone = group * cores
    first_chip = chips // 2 + chips // 8
    first_part = group - chips + first_chip
    feat_order = from_member(first_chip * cores, groups)
    part_order = from_member(first_part, group)
    every_order = from_member(first_part * cores, everyone)
    apart_order = from_member(others // 2, others)
    lists = (16, node_rows)
    loads = (
        features, neighbours_one.T, counts_one[None, :], self_one, neigh_one, neighbours_two.T,
        counts_two[None, :], cotangent, bias_one[None, :], bias_two[None, :],
    )
    chunks, send, biases = pl.pallas_call(
        functools.partial(pick_kernel, feat_order),
        out_shape=(
            jax.ShapeDtypeStruct((groups, 2 * rows, span + hid), jnp.bfloat16),
            jax.ShapeDtypeStruct((node_rows + lists[0], hid), jnp.bfloat16),
            jax.ShapeDtypeStruct((2, hid), jnp.float32),
        ),
        in_specs=[pl.BlockSpec(memory_space=pltpu.HBM)] * len(loads),
        scratch_shapes=[pltpu.VMEM(load.shape, load.dtype) for load in loads]
        + [
            pltpu.VMEM((2 * rows, batch_nodes), jnp.float32),
            pltpu.VMEM((4 * rows, batch_nodes), jnp.bfloat16),
            pltpu.VMEM((2 * rows, batch_nodes + 2 * node_rows), jnp.float32),
            pltpu.VMEM(lists, jnp.int32),
            pltpu.SemaphoreType.DMA((len(loads),)),
        ],
        compiler_params=pltpu.CompilerParams(vmem_limit_bytes=PICK_VMEM_BYTES),
        name="pick",
    )(*loads)
    got = lax.all_to_all(
        chunks, ("chip", "core"), 0, 0, tiled=True, axis_index_groups=[feat_order]
    )
    other = lax.ppermute(send, "core", [(0, 1), (1, 0)])
    place = jnp.stack([lax.axis_index("core"), lax.axis_index("chip") * cores - 1])
    hidden_two, parts = pl.pallas_call(
        functools.partial(layers_kernel, neighbours_two.shape[1]),
        out_shape=(
            jax.ShapeDtypeStruct((node_rows, hid), jnp.bfloat16),
            jax.ShapeDtypeStruct((group, 9, 2, LANES), jnp.float32),
        ),
        in_specs=[pl.BlockSpec(memory_space=pltpu.SMEM)]
        + [pl.BlockSpec(memory_space=pltpu.VMEM)] * 6,
        compiler_params=params,
        name="layers",
    )(place, got.reshape(groups * 2 * rows, span + hid), send, other, biases, self_two, neigh_two)
    inner = lax.all_to_all(
        parts, ("pair", "chip"), 0, 0, tiled=True, axis_index_groups=[part_order]
    ).sum(axis=0)
    spread = jnp.broadcast_to(inner[None], (others,) + inner.shape)
    total = lax.all_to_all(
        spread, "apart", 0, 0, tiled=True, axis_index_groups=[apart_order]
    ).sum(axis=0)
    total = total.reshape(18, LANES) * (1.0 / (batch_nodes * pairs * others))
    spread = pl.pallas_call(
        repeat_kernel,
        out_shape=jax.ShapeDtypeStruct((everyone, hid // group, hid), jnp.bfloat16),
        compiler_params=params,
        name="repeat",
    )(total)
    whole = lax.all_to_all(
        spread, ("pair", "chip", "core"), 0, 0, tiled=True, axis_index_groups=[every_order]
    )
    grad_self, grad_neigh = pl.pallas_call(
        widen_kernel,
        out_shape=(jax.ShapeDtypeStruct((hid, hid), jnp.float32),) * 2,
        compiler_params=params,
        name="widen",
    )(whole.reshape(group, cores, hid // group, hid))
    return hidden_two, grad_self, grad_neigh, total[16:].reshape(hid)


def solution(mesh):
    replicas, groups = mesh.devices.shape
    split = Mesh(
        mesh.devices.reshape(replicas // 2, 2, groups // 2, 2), ("apart", "pair", "chip", "core")
    )
    dp = ("apart", "pair")
    feat = ("chip", "core")
    every = dp + feat
    return jax.shard_map(
        local,
        mesh=split,
        in_specs=(
            P(feat, dp),
            P(dp, None),
            P(dp),
            P(every, None),
            P(every),
            P(feat, None),
            P(feat, None),
            P(),
            P(),
            P(),
            P(),
            P(every, None),
        ),
        out_specs=(P(every, None), P(), P(), P()),
        check_vma=False,
    )
```

```python
import functools
import math

import jax
import jax.numpy as jnp
from jax import lax
from jax.experimental import pallas as pl
from jax.experimental.pallas import tpu as pltpu
from jax.sharding import Mesh
from jax.sharding import PartitionSpec as P

LANES = 128
DEAD = -64
INNER = math.sqrt(2.0 / math.pi)
CUBIC = 0.044715
VMEM_BYTES = 48 * 1024 * 1024
PICK_VMEM_BYTES = 57_000_000


WITHIN = lax.GatherDimensionNumbers(
    offset_dims=(),
    collapsed_slice_dims=(1,),
    start_index_map=(1,),
    operand_batching_dims=(0,),
    start_indices_batching_dims=(0,),
)


def lane_gather(table, lane):
    return lax.gather(
        table, lane[..., None], WITHIN, (1, 1), mode=lax.GatherScatterMode.PROMISE_IN_BOUNDS
    )


def pick_kernel(
    order, feats_hbm, ids_hbm, counts_hbm, self_hbm, neigh_hbm, ids_two_hbm, counts_two_hbm,
    cot_hbm, bias_one_hbm, bias_two_hbm, out_ref, send_ref, biases_ref,
    feats_ref, ids_ref, counts_ref, self_ref, neigh_ref, ids_two_ref, counts_two_ref, cot_ref,
    bias_one_ref, bias_two_ref, wide, table, sums, lists, arrived,
):
    copies = [
        pltpu.make_async_copy(source, target, arrived.at[i])
        for i, (source, target) in enumerate(
            (
                (feats_hbm, feats_ref),
                (ids_hbm, ids_ref),
                (counts_hbm, counts_ref),
                (self_hbm, self_ref),
                (neigh_hbm, neigh_ref),
                (ids_two_hbm, ids_two_ref),
                (counts_two_hbm, counts_two_ref),
                (cot_hbm, cot_ref),
                (bias_one_hbm, bias_one_ref),
                (bias_two_hbm, bias_two_ref),
            )
        )
    ]
    for copy in copies:
        copy.start()
    rows, nodes = feats_ref.shape
    fan = ids_ref.shape[0]
    blocks = nodes // LANES
    copies[0].wait()
    values = feats_ref[...].astype(jnp.float32)
    wide[0:rows, :] = values
    wide[rows : 2 * rows, :] = values
    table[...] = jnp.concatenate([wide[...]] * 2, axis=0).astype(jnp.bfloat16)
    for copy in copies[1:]:
        copy.wait()
    row = lax.broadcasted_iota(jnp.int32, (4 * rows, LANES), 0)
    upper = lax.broadcasted_iota(jnp.int32, (2 * rows, LANES), 0) < rows

    def four_blocks(quad, carry):
        start = pl.multiple_of(quad * 4 * LANES, 4 * LANES)

        def spread(ref, k):
            parts = [
                jnp.broadcast_to(ref[k : k + 1, pl.ds(start + i * LANES, LANES)], row.shape)
                for i in range(4)
            ]
            return jnp.where(
                row < 2 * rows,
                jnp.where(row < rows, parts[0], parts[1]),
                jnp.where(row < 3 * rows, parts[2], parts[3]),
            )

        counts = spread(counts_ref, 0)
        total = jnp.zeros(row.shape, jnp.float32)
        for k in range(fan):
            ids = spread(ids_ref, k)
            lane = jnp.bitwise_and(ids, LANES - 1).astype(jnp.int16)
            block = lax.shift_right_logical(ids, 7).astype(jnp.int16)
            level = [
                lane_gather(table[:, j * LANES : (j + 1) * LANES], lane) for j in range(blocks)
            ]
            bit = 1
            while len(level) > 1:
                odd = jnp.bitwise_and(block, jnp.int16(bit)) != 0
                level = [
                    jnp.where(odd, level[i + 1], level[i]) for i in range(0, len(level), 2)
                ]
                bit *= 2
            total = total + jnp.where(counts > k, level[0].astype(jnp.float32), 0.0)
        mean = total / counts.astype(jnp.float32)
        for i in range(4):
            half = mean[(i // 2) * 2 * rows : (i // 2 + 1) * 2 * rows]
            if i % 2 == 0:
                half = pltpu.roll(half, rows, axis=0)
            to = pl.multiple_of(start + (i + 1) * LANES, LANES)
            sums[:, pl.ds(to, LANES)] = jnp.where(
                upper, wide[:, pl.ds(start + i * LANES, LANES)], half
            )
        return carry

    lax.fori_loop(0, blocks // 4, four_blocks, 0, unroll=True)
    sums[:, 0:LANES] = sums[:, blocks * LANES : (blocks + 1) * LANES]
    sums[:, (blocks + 1) * LANES :] = sums[:, LANES : 2 * LANES]
    node_rows = cot_ref.shape[0]
    fan_two = ids_two_ref.shape[0]
    lists[...] = jnp.zeros_like(lists)
    lists[0:fan_two, :] = ids_two_ref[...]
    row = lax.broadcasted_iota(jnp.int32, lists.shape, 0)
    counts_two = jnp.broadcast_to(counts_two_ref[...], lists.shape)
    place = jnp.bitwise_and(lists[...], LANES - 1)
    block = jnp.where(row < counts_two, lax.shift_right_logical(lists[...], 7), DEAD)
    place = jnp.where(row == fan_two, counts_two, place)
    send_ref[0:node_rows, :] = cot_ref[...]
    send_ref[node_rows:, 0:LANES] = place.astype(jnp.float32).astype(jnp.bfloat16)
    send_ref[node_rows:, LANES:] = block.astype(jnp.float32).astype(jnp.bfloat16)
    biases_ref[0:1, :] = bias_one_ref[...]
    biases_ref[1:2, :] = bias_two_ref[...]
    weights = jnp.concatenate(
        [self_ref[...].astype(jnp.float32), neigh_ref[...].astype(jnp.float32)], axis=0
    ).astype(jnp.bfloat16)
    for first in range(0, blocks, 2):
        span = sums[:, first * LANES : (first + 4) * LANES].astype(jnp.bfloat16)
        for block in (first, first + 1):
            to = order.index(block)
            out_ref[to, :, 0 : 4 * LANES] = span
            out_ref[to, :, 4 * LANES :] = weights


def gelu_parts(value):
    square = value * value
    bent = jnp.tanh(INNER * (value + CUBIC * (value * square)))
    half = 0.5 * (1.0 + bent)
    slope = half + 0.5 * value * (1.0 - bent * bent) * (INNER * (1.0 + 3.0 * CUBIC * square))
    return value * half, slope


def lists_kernel(
    fan, place_ref, own_ref, other_ref, bias_ref, often_ref, counts_ref, cot_ref, biases_ref
):
    span, node_rows = often_ref.shape[0], often_ref.shape[1] // 2
    is_first = jnp.bitwise_and(place_ref[0], 1) == 0
    first_block = lax.shift_right_logical(place_ref[0], 1) * 2 - 1

    def lists_of(ref):
        kept = ref[node_rows:, :].astype(jnp.float32)
        place = kept[:, :LANES]
        numbers = (kept[:, LANES:].astype(jnp.int32) - first_block) * LANES + place.astype(jnp.int32)
        return numbers, place

    biases_ref[...] = bias_ref[...]
    own, other = lists_of(own_ref), lists_of(other_ref)
    number = lax.broadcasted_iota(jnp.int32, (span, node_rows), 0).astype(jnp.int16)
    one, zero = jnp.ones((), jnp.bfloat16), jnp.zeros((), jnp.bfloat16)
    own_cot, other_cot = own_ref[0:node_rows, :], other_ref[0:node_rows, :]
    for block in range(2):
        nodes = slice(block * node_rows, (block + 1) * node_rows)
        is_own = is_first if block == 0 else jnp.logical_not(is_first)
        numbers, places = (jnp.where(is_own, mine, its) for mine, its in zip(own, other))
        total = jnp.zeros((span, node_rows), jnp.bfloat16)
        for k in range(fan):
            ids = jnp.broadcast_to(numbers[k : k + 1, :], (span, node_rows)).astype(jnp.int16)
            total = total + jnp.where(ids == number, one, zero)
        often_ref[:, nodes] = total
        counts_ref[nodes, :] = jnp.broadcast_to(places[fan : fan + 1, :], (LANES, LANES)).T
        cot_ref[nodes, :] = jnp.where(is_own, own_cot, other_cot)


def layers_kernel(
    place_ref, got_ref, often_ref, counts_ref, cot_ref, bias_ref, self_ref, neigh_ref,
    hidden_hbm, parts_ref, hidden_ref, left,
):
    node_rows, hid = hidden_ref.shape
    span = 4 * node_rows
    over_rows = (((0,), (0,)), ((), ()))
    is_first = jnp.bitwise_and(place_ref[0], 1) == 0
    got = got_ref[...]
    pre_one = lax.dot_general(
        got[:, :span], got[:, span:], over_rows, preferred_element_type=jnp.float32
    )
    hidden = gelu_parts(pre_one + bias_ref[0:1, :])[0].astype(jnp.bfloat16)
    own = hidden[node_rows : 3 * node_rows]
    summed = lax.dot_general(
        often_ref[...], hidden, over_rows, preferred_element_type=jnp.float32
    )
    counts = jnp.concatenate([counts_ref[...]] * (hid // LANES), axis=1)
    agg = (summed / counts).astype(jnp.bfloat16)
    pre_two = jnp.dot(own, self_ref[...], preferred_element_type=jnp.float32)
    pre_two = pre_two + jnp.dot(agg, neigh_ref[...], preferred_element_type=jnp.float32)
    value, slope = gelu_parts(pre_two + bias_ref[1:2, :])
    hidden_ref[...] = jnp.where(is_first, value[:node_rows], value[node_rows:]).astype(jnp.bfloat16)
    copy = pltpu.make_async_copy(hidden_ref, hidden_hbm, left)
    copy.start()
    delta = (cot_ref[...].astype(jnp.float32) * slope).astype(jnp.bfloat16)
    rows = jnp.where(is_first, own, agg)
    grads = lax.dot_general(rows, delta, over_rows, preferred_element_type=jnp.float32)
    bias = jnp.sum(delta.astype(jnp.float32), axis=0, keepdims=True)
    for half in range(2):
        columns = slice(half * LANES, (half + 1) * LANES)
        for part in range(parts_ref.shape[0]):
            parts_ref[part, 4 * half : 4 * half + 4] = grads[
                part * 8 : part * 8 + 8, columns
            ].reshape(4, 2, LANES)
            parts_ref[part, 8, half : half + 1, :] = bias[:, columns]
    copy.wait()


def repeat_kernel(part_ref, out_ref):
    part = jnp.concatenate([part_ref[0:8, :], part_ref[8:16, :]], axis=1).astype(jnp.bfloat16)
    for to in range(out_ref.shape[0]):
        out_ref[to] = part


def widen_kernel(got_ref, self_ref, neigh_ref):
    parts, _, rows, _ = got_ref.shape
    for part in range(parts):
        self_ref[part * rows : (part + 1) * rows, :] = got_ref[part, 0].astype(jnp.float32)
        neigh_ref[part * rows : (part + 1) * rows, :] = got_ref[part, 1].astype(jnp.float32)


def from_member(first, size):
    return [(first + i) % size for i in range(size)]


def local(
    features,
    neighbours_one,
    counts_one,
    neighbours_two,
    counts_two,
    self_one,
    neigh_one,
    bias_one,
    self_two,
    neigh_two,
    bias_two,
    cotangent,
):
    rows, batch_nodes = features.shape
    pairs, chips, cores = lax.axis_size("pair"), lax.axis_size("chip"), lax.axis_size("core")
    others = lax.axis_size("apart")
    groups = chips * cores
    node_rows = batch_nodes // groups
    hid = self_one.shape[1]
    span = 4 * node_rows
    params = pltpu.CompilerParams(vmem_limit_bytes=VMEM_BYTES)
    group = pairs * chips
    everyone = group * cores
    first_chip = chips // 2 + chips // 8
    first_part = group - chips + first_chip
    feat_order = from_member(first_chip * cores, groups)
    part_order = from_member(first_part, group)
    every_order = from_member(first_part * cores, everyone)
    apart_order = from_member(others // 2, others)
    lists = (16, node_rows)
    loads = (
        features, neighbours_one.T, counts_one[None, :], self_one, neigh_one, neighbours_two.T,
        counts_two[None, :], cotangent, bias_one[None, :], bias_two[None, :],
    )
    chunks, send, biases = pl.pallas_call(
        functools.partial(pick_kernel, feat_order),
        out_shape=(
            jax.ShapeDtypeStruct((groups, 2 * rows, span + hid), jnp.bfloat16),
            jax.ShapeDtypeStruct((node_rows + lists[0], hid), jnp.bfloat16),
            jax.ShapeDtypeStruct((2, hid), jnp.float32),
        ),
        in_specs=[pl.BlockSpec(memory_space=pltpu.HBM)] * len(loads),
        scratch_shapes=[pltpu.VMEM(load.shape, load.dtype) for load in loads]
        + [
            pltpu.VMEM((2 * rows, batch_nodes), jnp.float32),
            pltpu.VMEM((4 * rows, batch_nodes), jnp.bfloat16),
            pltpu.VMEM((2 * rows, batch_nodes + 2 * node_rows), jnp.float32),
            pltpu.VMEM(lists, jnp.int32),
            pltpu.SemaphoreType.DMA((len(loads),)),
        ],
        compiler_params=pltpu.CompilerParams(vmem_limit_bytes=PICK_VMEM_BYTES),
        name="pick",
    )(*loads)
    got = lax.all_to_all(
        chunks, ("chip", "core"), 0, 0, tiled=True, axis_index_groups=[feat_order]
    )
    other = lax.ppermute(send, "core", [(0, 1), (1, 0)])
    place = lax.axis_index(("chip", "core"))[None]
    scalar = pl.BlockSpec(memory_space=pltpu.SMEM)
    array = pl.BlockSpec(memory_space=pltpu.VMEM)
    often, counts, cot, biases = pl.pallas_call(
        functools.partial(lists_kernel, neighbours_two.shape[1]),
        out_shape=(
            jax.ShapeDtypeStruct((span, 2 * node_rows), jnp.bfloat16),
            jax.ShapeDtypeStruct((2 * node_rows, LANES), jnp.float32),
            jax.ShapeDtypeStruct((2 * node_rows, hid), jnp.bfloat16),
            jax.ShapeDtypeStruct(biases.shape, jnp.float32),
        ),
        in_specs=[scalar, array, array, array],
        compiler_params=params,
        name="lists",
    )(place, send, other, biases)
    hidden_two, parts = pl.pallas_call(
        layers_kernel,
        out_shape=(
            jax.ShapeDtypeStruct((node_rows, hid), jnp.bfloat16),
            jax.ShapeDtypeStruct((group, 9, 2, LANES), jnp.float32),
        ),
        in_specs=[scalar] + [array] * 7,
        out_specs=(pl.BlockSpec(memory_space=pltpu.HBM), array),
        scratch_shapes=[pltpu.VMEM((node_rows, hid), jnp.bfloat16), pltpu.SemaphoreType.DMA],
        compiler_params=params,
        name="layers",
    )(
        place, got.reshape(groups * 2 * rows, span + hid), often, counts, cot, biases, self_two,
        neigh_two,
    )
    inner = lax.all_to_all(
        parts, ("pair", "chip"), 0, 0, tiled=True, axis_index_groups=[part_order]
    ).sum(axis=0)
    spread = jnp.broadcast_to(inner[None], (others,) + inner.shape)
    total = lax.all_to_all(
        spread, "apart", 0, 0, tiled=True, axis_index_groups=[apart_order]
    ).sum(axis=0)
    total = total.reshape(18, LANES) * (1.0 / (batch_nodes * pairs * others))
    spread = pl.pallas_call(
        repeat_kernel,
        out_shape=jax.ShapeDtypeStruct((everyone, hid // group, hid), jnp.bfloat16),
        compiler_params=params,
        name="repeat",
    )(total)
    whole = lax.all_to_all(
        spread, ("pair", "chip", "core"), 0, 0, tiled=True, axis_index_groups=[every_order]
    )
    grad_self, grad_neigh = pl.pallas_call(
        widen_kernel,
        out_shape=(jax.ShapeDtypeStruct((hid, hid), jnp.float32),) * 2,
        compiler_params=params,
        name="widen",
    )(whole.reshape(group, cores, hid // group, hid))
    return hidden_two, grad_self, grad_neigh, total[16:].reshape(hid)


def solution(mesh):
    replicas, groups = mesh.devices.shape
    split = Mesh(
        mesh.devices.reshape(replicas // 2, 2, groups // 2, 2), ("apart", "pair", "chip", "core")
    )
    dp = ("apart", "pair")
    feat = ("chip", "core")
    every = dp + feat
    return jax.shard_map(
        local,
        mesh=split,
        in_specs=(
            P(feat, dp),
            P(dp, None),
            P(dp),
            P(every, None),
            P(every),
            P(feat, None),
            P(feat, None),
            P(),
            P(),
            P(),
            P(),
            P(every, None),
        ),
        out_specs=(P(every, None), P(), P(), P()),
        check_vma=False,
    )
```

```python
import functools
import math

import jax
import jax.numpy as jnp
from jax import lax
from jax.experimental import pallas as pl
from jax.experimental.pallas import tpu as pltpu
from jax.sharding import Mesh
from jax.sharding import PartitionSpec as P

LANES = 128
DEAD = -64
INNER = math.sqrt(2.0 / math.pi)
CUBIC = 0.044715
VMEM_BYTES = 48 * 1024 * 1024
PICK_VMEM_BYTES = 57_000_000


WITHIN = lax.GatherDimensionNumbers(
    offset_dims=(),
    collapsed_slice_dims=(1,),
    start_index_map=(1,),
    operand_batching_dims=(0,),
    start_indices_batching_dims=(0,),
)


def lane_gather(table, lane):
    return lax.gather(
        table, lane[..., None], WITHIN, (1, 1), mode=lax.GatherScatterMode.PROMISE_IN_BOUNDS
    )


def pick_kernel(
    order, feats_hbm, ids_hbm, counts_hbm, self_hbm, neigh_hbm, ids_two_hbm, counts_two_hbm,
    cot_hbm, bias_one_hbm, bias_two_hbm, out_ref, send_ref, biases_ref,
    feats_ref, ids_ref, counts_ref, self_ref, neigh_ref, ids_two_ref, counts_two_ref, cot_ref,
    bias_one_ref, bias_two_ref, wide, table, sums, lists, arrived,
):
    copies = [
        pltpu.make_async_copy(source, target, arrived.at[i])
        for i, (source, target) in enumerate(
            (
                (feats_hbm, feats_ref),
                (ids_hbm, ids_ref),
                (counts_hbm, counts_ref),
                (self_hbm, self_ref),
                (neigh_hbm, neigh_ref),
                (ids_two_hbm, ids_two_ref),
                (counts_two_hbm, counts_two_ref),
                (cot_hbm, cot_ref),
                (bias_one_hbm, bias_one_ref),
                (bias_two_hbm, bias_two_ref),
            )
        )
    ]
    for copy in copies:
        copy.start()
    rows, nodes = feats_ref.shape
    fan = ids_ref.shape[0]
    blocks = nodes // LANES
    copies[0].wait()
    values = feats_ref[...].astype(jnp.float32)
    wide[0:rows, :] = values
    wide[rows : 2 * rows, :] = values
    table[...] = jnp.concatenate([wide[...]] * 2, axis=0).astype(jnp.bfloat16)
    for copy in copies[1:]:
        copy.wait()
    row = lax.broadcasted_iota(jnp.int32, (4 * rows, LANES), 0)
    upper = lax.broadcasted_iota(jnp.int32, (2 * rows, LANES), 0) < rows

    def four_blocks(quad, carry):
        start = pl.multiple_of(quad * 4 * LANES, 4 * LANES)

        def spread(ref, k):
            parts = [
                jnp.broadcast_to(ref[k : k + 1, pl.ds(start + i * LANES, LANES)], row.shape)
                for i in range(4)
            ]
            return jnp.where(
                row < 2 * rows,
                jnp.where(row < rows, parts[0], parts[1]),
                jnp.where(row < 3 * rows, parts[2], parts[3]),
            )

        counts = spread(counts_ref, 0)
        total = jnp.zeros(row.shape, jnp.float32)
        for k in range(fan):
            ids = spread(ids_ref, k)
            lane = jnp.bitwise_and(ids, LANES - 1).astype(jnp.int16)
            block = lax.shift_right_logical(ids, 7).astype(jnp.int16)
            level = [
                lane_gather(table[:, j * LANES : (j + 1) * LANES], lane) for j in range(blocks)
            ]
            bit = 1
            while len(level) > 1:
                odd = jnp.bitwise_and(block, jnp.int16(bit)) != 0
                level = [
                    jnp.where(odd, level[i + 1], level[i]) for i in range(0, len(level), 2)
                ]
                bit *= 2
            total = total + jnp.where(counts > k, level[0].astype(jnp.float32), 0.0)
        mean = total / counts.astype(jnp.float32)
        for i in range(4):
            half = mean[(i // 2) * 2 * rows : (i // 2 + 1) * 2 * rows]
            if i % 2 == 0:
                half = pltpu.roll(half, rows, axis=0)
            to = pl.multiple_of(start + (i + 1) * LANES, LANES)
            sums[:, pl.ds(to, LANES)] = jnp.where(
                upper, wide[:, pl.ds(start + i * LANES, LANES)], half
            )
        return carry

    lax.fori_loop(0, blocks // 4, four_blocks, 0, unroll=True)
    sums[:, 0:LANES] = sums[:, blocks * LANES : (blocks + 1) * LANES]
    sums[:, (blocks + 1) * LANES :] = sums[:, LANES : 2 * LANES]
    node_rows = cot_ref.shape[0]
    fan_two = ids_two_ref.shape[0]
    lists[...] = jnp.zeros_like(lists)
    lists[0:fan_two, :] = ids_two_ref[...]
    row = lax.broadcasted_iota(jnp.int32, lists.shape, 0)
    counts_two = jnp.broadcast_to(counts_two_ref[...], lists.shape)
    place = jnp.bitwise_and(lists[...], LANES - 1)
    block = jnp.where(row < counts_two, lax.shift_right_logical(lists[...], 7), DEAD)
    place = jnp.where(row == fan_two, counts_two, place)
    send_ref[0:node_rows, :] = cot_ref[...]
    send_ref[node_rows:, 0:LANES] = place.astype(jnp.float32).astype(jnp.bfloat16)
    send_ref[node_rows:, LANES:] = block.astype(jnp.float32).astype(jnp.bfloat16)
    biases_ref[0:1, :] = bias_one_ref[...]
    biases_ref[1:2, :] = bias_two_ref[...]
    weights = jnp.concatenate(
        [self_ref[...].astype(jnp.float32), neigh_ref[...].astype(jnp.float32)], axis=0
    ).astype(jnp.bfloat16)
    for first in range(0, blocks, 2):
        span = sums[:, first * LANES : (first + 4) * LANES].astype(jnp.bfloat16)
        for block in (first, first + 1):
            to = order.index(block)
            out_ref[to, :, 0 : 4 * LANES] = span
            out_ref[to, :, 4 * LANES :] = weights


def gelu_parts(value):
    square = value * value
    bent = jnp.tanh(INNER * (value + CUBIC * (value * square)))
    half = 0.5 * (1.0 + bent)
    slope = half + 0.5 * value * (1.0 - bent * bent) * (INNER * (1.0 + 3.0 * CUBIC * square))
    return value * half, slope


def lists_kernel(
    fan, place_ref, own_ref, other_ref, bias_ref, often_ref, counts_ref, cot_ref, biases_ref
):
    span, node_rows = often_ref.shape[1], often_ref.shape[0] // 2
    is_first = jnp.bitwise_and(place_ref[0], 1) == 0
    first_block = lax.shift_right_logical(place_ref[0], 1) * 2 - 1

    def lists_of(ref):
        kept = ref[node_rows:, :].astype(jnp.float32)
        place = kept[:, :LANES]
        numbers = (kept[:, LANES:].astype(jnp.int32) - first_block) * LANES + place.astype(jnp.int32)
        return numbers, place

    biases_ref[...] = bias_ref[...]
    own, other = lists_of(own_ref), lists_of(other_ref)
    number = lax.broadcasted_iota(jnp.int32, (span, node_rows), 0).astype(jnp.int16)
    one, zero = jnp.ones((), jnp.bfloat16), jnp.zeros((), jnp.bfloat16)
    own_cot, other_cot = own_ref[0:node_rows, :], other_ref[0:node_rows, :]
    for block in range(2):
        nodes = slice(block * node_rows, (block + 1) * node_rows)
        is_own = is_first if block == 0 else jnp.logical_not(is_first)
        numbers, places = (jnp.where(is_own, mine, its) for mine, its in zip(own, other))
        total = jnp.zeros((span, node_rows), jnp.bfloat16)
        for k in range(fan):
            ids = jnp.broadcast_to(numbers[k : k + 1, :], (span, node_rows)).astype(jnp.int16)
            total = total + jnp.where(ids == number, one, zero)
        often_ref[nodes, :] = total.T
        counts_ref[nodes, :] = jnp.broadcast_to(places[fan : fan + 1, :], (LANES, LANES)).T
        cot_ref[nodes, :] = jnp.where(is_own, own_cot, other_cot)


def layers_kernel(
    place_ref, got_ref, often_ref, counts_ref, cot_ref, bias_ref, self_ref, neigh_ref,
    hidden_hbm, parts_ref, hidden_ref, left,
):
    node_rows, hid = hidden_ref.shape
    span = 4 * node_rows
    over_rows = (((0,), (0,)), ((), ()))
    is_first = jnp.bitwise_and(place_ref[0], 1) == 0
    got = got_ref[...]
    pre_one = lax.dot_general(
        got[:, :span], got[:, span:], over_rows, preferred_element_type=jnp.float32
    )
    hidden = gelu_parts(pre_one + bias_ref[0:1, :])[0].astype(jnp.bfloat16)
    own = hidden[node_rows : 3 * node_rows]
    summed = jnp.dot(often_ref[...], hidden, preferred_element_type=jnp.float32)
    counts = jnp.concatenate([counts_ref[...]] * (hid // LANES), axis=1)
    agg = (summed / counts).astype(jnp.bfloat16)
    pre_two = jnp.dot(own, self_ref[...], preferred_element_type=jnp.float32)
    pre_two = pre_two + jnp.dot(agg, neigh_ref[...], preferred_element_type=jnp.float32)
    value, slope = gelu_parts(pre_two + bias_ref[1:2, :])
    hidden_ref[...] = jnp.where(is_first, value[:node_rows], value[node_rows:]).astype(jnp.bfloat16)
    copy = pltpu.make_async_copy(hidden_ref, hidden_hbm, left)
    copy.start()
    delta = (cot_ref[...].astype(jnp.float32) * slope).astype(jnp.bfloat16)
    rows = jnp.where(is_first, own, agg)
    grads = lax.dot_general(rows, delta, over_rows, preferred_element_type=jnp.float32)
    bias = jnp.sum(delta.astype(jnp.float32), axis=0, keepdims=True)
    for half in range(2):
        columns = slice(half * LANES, (half + 1) * LANES)
        for part in range(parts_ref.shape[0]):
            parts_ref[part, 4 * half : 4 * half + 4] = grads[
                part * 8 : part * 8 + 8, columns
            ].reshape(4, 2, LANES)
            parts_ref[part, 8, half : half + 1, :] = bias[:, columns]
    copy.wait()


def repeat_kernel(part_ref, out_ref):
    part = jnp.concatenate([part_ref[0:8, :], part_ref[8:16, :]], axis=1).astype(jnp.bfloat16)
    for to in range(out_ref.shape[0]):
        out_ref[to] = part


def widen_kernel(got_ref, total_ref, self_ref, neigh_ref, bias_ref):
    parts, _, rows, _ = got_ref.shape
    for part in range(parts):
        self_ref[part * rows : (part + 1) * rows, :] = got_ref[part, 1].astype(jnp.float32)
        neigh_ref[part * rows : (part + 1) * rows, :] = got_ref[part, 0].astype(jnp.float32)
    bias_ref[...] = jnp.concatenate([total_ref[16:17, :], total_ref[17:18, :]], axis=1)


def from_member(first, size):
    return [(first + i) % size for i in range(size)]


def both_cores(order):
    return [2 * chip + core for chip in order for core in (1, 0)]


def local(
    features,
    neighbours_one,
    counts_one,
    neighbours_two,
    counts_two,
    self_one,
    neigh_one,
    bias_one,
    self_two,
    neigh_two,
    bias_two,
    cotangent,
):
    rows, batch_nodes = features.shape
    pairs, chips, cores = lax.axis_size("pair"), lax.axis_size("chip"), lax.axis_size("core")
    others = lax.axis_size("apart")
    groups = chips * cores
    node_rows = batch_nodes // groups
    hid = self_one.shape[1]
    span = 4 * node_rows
    params = pltpu.CompilerParams(vmem_limit_bytes=VMEM_BYTES)
    group = pairs * chips
    everyone = group * cores
    first_chip = chips // 2 + chips // 8
    first_part = group - chips + first_chip
    feat_order = both_cores(from_member(first_chip, chips))
    part_order = from_member(first_part, group)
    every_order = both_cores(part_order)
    apart_order = from_member(others // 2, others)
    lists = (16, node_rows)
    loads = (
        features, neighbours_one.T, counts_one[None, :], self_one, neigh_one, neighbours_two.T,
        counts_two[None, :], cotangent, bias_one[None, :], bias_two[None, :],
    )
    chunks, send, biases = pl.pallas_call(
        functools.partial(pick_kernel, feat_order),
        out_shape=(
            jax.ShapeDtypeStruct((groups, 2 * rows, span + hid), jnp.bfloat16),
            jax.ShapeDtypeStruct((node_rows + lists[0], hid), jnp.bfloat16),
            jax.ShapeDtypeStruct((2, hid), jnp.float32),
        ),
        in_specs=[pl.BlockSpec(memory_space=pltpu.HBM)] * len(loads),
        scratch_shapes=[pltpu.VMEM(load.shape, load.dtype) for load in loads]
        + [
            pltpu.VMEM((2 * rows, batch_nodes), jnp.float32),
            pltpu.VMEM((4 * rows, batch_nodes), jnp.bfloat16),
            pltpu.VMEM((2 * rows, batch_nodes + 2 * node_rows), jnp.float32),
            pltpu.VMEM(lists, jnp.int32),
            pltpu.SemaphoreType.DMA((len(loads),)),
        ],
        compiler_params=pltpu.CompilerParams(vmem_limit_bytes=PICK_VMEM_BYTES),
        name="pick",
    )(*loads)
    got = lax.all_to_all(
        chunks, ("chip", "core"), 0, 0, tiled=True, axis_index_groups=[feat_order]
    )
    other = lax.ppermute(send, "core", [(0, 1), (1, 0)])
    place = lax.axis_index(("chip", "core"))[None]
    scalar = pl.BlockSpec(memory_space=pltpu.SMEM)
    array = pl.BlockSpec(memory_space=pltpu.VMEM)
    often, counts, cot, biases = pl.pallas_call(
        functools.partial(lists_kernel, neighbours_two.shape[1]),
        out_shape=(
            jax.ShapeDtypeStruct((2 * node_rows, span), jnp.bfloat16),
            jax.ShapeDtypeStruct((2 * node_rows, LANES), jnp.float32),
            jax.ShapeDtypeStruct((2 * node_rows, hid), jnp.bfloat16),
            jax.ShapeDtypeStruct(biases.shape, jnp.float32),
        ),
        in_specs=[scalar, array, array, array],
        compiler_params=params,
        name="lists",
    )(place, send, other, biases)
    hidden_two, parts = pl.pallas_call(
        layers_kernel,
        out_shape=(
            jax.ShapeDtypeStruct((node_rows, hid), jnp.bfloat16),
            jax.ShapeDtypeStruct((group, 9, 2, LANES), jnp.float32),
        ),
        in_specs=[scalar] + [array] * 7,
        out_specs=(pl.BlockSpec(memory_space=pltpu.HBM), array),
        scratch_shapes=[pltpu.VMEM((node_rows, hid), jnp.bfloat16), pltpu.SemaphoreType.DMA],
        compiler_params=params,
        name="layers",
    )(
        place, got.reshape(groups * 2 * rows, span + hid), often, counts, cot, biases, self_two,
        neigh_two,
    )
    inner = lax.all_to_all(
        parts, ("pair", "chip"), 0, 0, tiled=True, axis_index_groups=[part_order]
    ).sum(axis=0)
    spread = jnp.broadcast_to(inner[None], (others,) + inner.shape)
    total = lax.all_to_all(
        spread, "apart", 0, 0, tiled=True, axis_index_groups=[apart_order]
    ).sum(axis=0)
    total = total.reshape(18, LANES) * (1.0 / (batch_nodes * pairs * others))
    spread = pl.pallas_call(
        repeat_kernel,
        out_shape=jax.ShapeDtypeStruct((everyone, hid // group, hid), jnp.bfloat16),
        compiler_params=params,
        name="repeat",
    )(total)
    whole = lax.all_to_all(
        spread, ("pair", "chip", "core"), 0, 0, tiled=True, axis_index_groups=[every_order]
    )
    grad_self, grad_neigh, grad_bias = pl.pallas_call(
        widen_kernel,
        out_shape=(
            jax.ShapeDtypeStruct((hid, hid), jnp.float32),
            jax.ShapeDtypeStruct((hid, hid), jnp.float32),
            jax.ShapeDtypeStruct((1, hid), jnp.float32),
        ),
        compiler_params=params,
        name="widen",
    )(whole.reshape(group, cores, hid // group, hid), total)
    return hidden_two, grad_self, grad_neigh, grad_bias.reshape(hid)


def solution(mesh):
    replicas, groups = mesh.devices.shape
    split = Mesh(
        mesh.devices.reshape(replicas // 2, 2, groups // 2, 2), ("apart", "pair", "chip", "core")
    )
    dp = ("apart", "pair")
    feat = ("chip", "core")
    every = dp + feat
    return jax.shard_map(
        local,
        mesh=split,
        in_specs=(
            P(feat, dp),
            P(dp, None),
            P(dp),
            P(every, None),
            P(every),
            P(feat, None),
            P(feat, None),
            P(),
            P(),
            P(),
            P(),
            P(every, None),
        ),
        out_specs=(P(every, None), P(), P(), P()),
        check_vma=False,
    )
```

```python
import functools
import math

import jax
import jax.numpy as jnp
from jax import lax
from jax.experimental import pallas as pl
from jax.experimental.pallas import tpu as pltpu
from jax.sharding import Mesh
from jax.sharding import PartitionSpec as P

LANES = 128
BY_MATMUL = 8
REACH = 256
DEAD = -64
INNER = math.sqrt(2.0 / math.pi)
CUBIC = 0.044715
VMEM_BYTES = 48 * 1024 * 1024
PICK_VMEM_BYTES = 57_000_000


WITHIN = lax.GatherDimensionNumbers(
    offset_dims=(),
    collapsed_slice_dims=(1,),
    start_index_map=(1,),
    operand_batching_dims=(0,),
    start_indices_batching_dims=(0,),
)


def lane_gather(table, lane):
    return lax.gather(
        table, lane[..., None], WITHIN, (1, 1), mode=lax.GatherScatterMode.PROMISE_IN_BOUNDS
    )


def pick_kernel(
    order, feats_hbm, ids_hbm, counts_hbm, self_hbm, neigh_hbm, ids_two_hbm, counts_two_hbm,
    cot_hbm, bias_one_hbm, bias_two_hbm, out_ref, send_ref, biases_ref,
    feats_ref, ids_ref, counts_ref, self_ref, neigh_ref, ids_two_ref, counts_two_ref, cot_ref,
    bias_one_ref, bias_two_ref, wide, table, sums, lists, arrived,
):
    copies = [
        pltpu.make_async_copy(source, target, arrived.at[i])
        for i, (source, target) in enumerate(
            (
                (feats_hbm, feats_ref),
                (ids_hbm, ids_ref),
                (counts_hbm, counts_ref),
                (self_hbm, self_ref),
                (neigh_hbm, neigh_ref),
                (ids_two_hbm, ids_two_ref),
                (counts_two_hbm, counts_two_ref),
                (cot_hbm, cot_ref),
                (bias_one_hbm, bias_one_ref),
                (bias_two_hbm, bias_two_ref),
            )
        )
    ]
    for copy in copies:
        copy.start()
    rows, nodes = feats_ref.shape
    fan = ids_ref.shape[0]
    blocks = nodes // LANES
    copies[0].wait()
    values = feats_ref[...].astype(jnp.float32)
    wide[0:rows, :] = values
    wide[rows : 2 * rows, :] = values
    table[...] = jnp.concatenate([wide[...]] * 2, axis=0).astype(jnp.bfloat16)
    reaches = nodes // REACH
    flat = jnp.concatenate(
        [values[:, i * REACH : (i + 1) * REACH] for i in range(reaches)], axis=0
    ).astype(jnp.bfloat16)
    for copy in copies[1:3]:
        copy.wait()
    in_reach = lax.broadcasted_iota(jnp.int32, (REACH, LANES), 0).astype(jnp.int16)
    reach_of_row = lax.broadcasted_iota(jnp.int32, (reaches * rows, LANES), 0) // rows
    one, zero = jnp.ones((), jnp.bfloat16), jnp.zeros((), jnp.bfloat16)
    row = lax.broadcasted_iota(jnp.int32, (4 * rows, LANES), 0)
    upper = lax.broadcasted_iota(jnp.int32, (2 * rows, LANES), 0) < rows

    def four_blocks(quad, carry):
        start = pl.multiple_of(quad * 4 * LANES, 4 * LANES)

        def spread(ref, k):
            parts = [
                jnp.broadcast_to(ref[k : k + 1, pl.ds(start + i * LANES, LANES)], row.shape)
                for i in range(4)
            ]
            return jnp.where(
                row < 2 * rows,
                jnp.where(row < rows, parts[0], parts[1]),
                jnp.where(row < 3 * rows, parts[2], parts[3]),
            )

        def by_lanes(k):
            ids = spread(ids_ref, k).astype(jnp.int16)
            lane = jnp.bitwise_and(ids, jnp.int16(LANES - 1))
            level = [
                lane_gather(table[:, j * LANES : (j + 1) * LANES], lane) for j in range(blocks)
            ]
            bit = LANES
            while len(level) > 1:
                odd = jnp.bitwise_and(ids, jnp.int16(bit)) != 0
                level = [
                    jnp.where(odd, level[i + 1], level[i]) for i in range(0, len(level), 2)
                ]
                bit *= 2
            return jnp.where(counts > k, level[0].astype(jnp.float32), 0.0)

        def by_matmul(k, i):
            lanes = pl.ds(start + i * LANES, LANES)
            ids, live = ids_ref[k : k + 1, lanes], counts_ref[0:1, lanes] > k
            place = jnp.broadcast_to(jnp.bitwise_and(ids, REACH - 1), in_reach.shape)
            hot = jnp.where(place.astype(jnp.int16) == in_reach, one, zero)
            found = jnp.dot(flat, hot, preferred_element_type=jnp.float32)
            reach = jnp.where(live, lax.shift_right_logical(ids, REACH.bit_length() - 1), -1)
            found = jnp.where(jnp.broadcast_to(reach, found.shape) == reach_of_row, found, 0.0)
            return jnp.sum(found.reshape(-1, 2 * rows, LANES), axis=0)

        counts = spread(counts_ref, 0)
        total = jnp.zeros(row.shape, jnp.float32)
        pairs = [jnp.zeros(upper.shape, jnp.float32)] * 4
        by_lane = fan - BY_MATMUL
        for k in range(max(by_lane, BY_MATMUL)):
            if k < by_lane:
                total = total + by_lanes(k)
            if k < BY_MATMUL:
                pairs = [pair + by_matmul(by_lane + k, i) for i, pair in enumerate(pairs)]
        pairs = [pair + pltpu.roll(pair, rows, axis=0) for pair in pairs]
        total = total + jnp.concatenate(
            [jnp.where(upper, pairs[i], pairs[i + 1]) for i in (0, 2)], axis=0
        )
        mean = total / counts.astype(jnp.float32)
        for i in range(4):
            half = mean[(i // 2) * 2 * rows : (i // 2 + 1) * 2 * rows]
            if i % 2 == 0:
                half = pltpu.roll(half, rows, axis=0)
            to = pl.multiple_of(start + (i + 1) * LANES, LANES)
            sums[:, pl.ds(to, LANES)] = jnp.where(
                upper, wide[:, pl.ds(start + i * LANES, LANES)], half
            )
        return carry

    lax.fori_loop(0, blocks // 4, four_blocks, 0, unroll=True)
    sums[:, 0:LANES] = sums[:, blocks * LANES : (blocks + 1) * LANES]
    sums[:, (blocks + 1) * LANES :] = sums[:, LANES : 2 * LANES]
    for copy in copies[3:]:
        copy.wait()
    node_rows = cot_ref.shape[0]
    fan_two = ids_two_ref.shape[0]
    lists[...] = jnp.zeros_like(lists)
    lists[0:fan_two, :] = ids_two_ref[...]
    row = lax.broadcasted_iota(jnp.int32, lists.shape, 0)
    counts_two = jnp.broadcast_to(counts_two_ref[...], lists.shape)
    place = jnp.bitwise_and(lists[...], LANES - 1)
    block = jnp.where(row < counts_two, lax.shift_right_logical(lists[...], 7), DEAD)
    place = jnp.where(row == fan_two, counts_two, place)
    send_ref[0:node_rows, :] = cot_ref[...]
    send_ref[node_rows:, 0:LANES] = place.astype(jnp.float32).astype(jnp.bfloat16)
    send_ref[node_rows:, LANES:] = block.astype(jnp.float32).astype(jnp.bfloat16)
    biases_ref[0:1, :] = bias_one_ref[...]
    biases_ref[1:2, :] = bias_two_ref[...]
    weights = jnp.concatenate(
        [self_ref[...].astype(jnp.float32), neigh_ref[...].astype(jnp.float32)], axis=0
    ).astype(jnp.bfloat16)
    for first in range(0, blocks, 2):
        span = sums[:, first * LANES : (first + 4) * LANES].astype(jnp.bfloat16)
        for block in (first, first + 1):
            to = order.index(block)
            out_ref[to, :, 0 : 4 * LANES] = span
            out_ref[to, :, 4 * LANES :] = weights


def gelu_parts(value):
    square = value * value
    bent = jnp.tanh(INNER * (value + CUBIC * (value * square)))
    half = 0.5 * (1.0 + bent)
    slope = half + 0.5 * value * (1.0 - bent * bent) * (INNER * (1.0 + 3.0 * CUBIC * square))
    return value * half, slope


def lists_kernel(
    fan, place_ref, own_ref, other_ref, bias_ref, often_ref, counts_ref, cot_ref, biases_ref
):
    span, node_rows = often_ref.shape[1], often_ref.shape[0] // 2
    is_first = jnp.bitwise_and(place_ref[0], 1) == 0
    first_block = lax.shift_right_logical(place_ref[0], 1) * 2 - 1

    def lists_of(ref):
        kept = ref[node_rows:, :].astype(jnp.float32)
        place = kept[:, :LANES]
        numbers = (kept[:, LANES:].astype(jnp.int32) - first_block) * LANES + place.astype(jnp.int32)
        return numbers, place

    biases_ref[...] = bias_ref[...]
    own, other = lists_of(own_ref), lists_of(other_ref)
    number = lax.broadcasted_iota(jnp.int32, (span, node_rows), 0).astype(jnp.int16)
    one, zero = jnp.ones((), jnp.bfloat16), jnp.zeros((), jnp.bfloat16)
    own_cot, other_cot = own_ref[0:node_rows, :], other_ref[0:node_rows, :]
    for block in range(2):
        nodes = slice(block * node_rows, (block + 1) * node_rows)
        is_own = is_first if block == 0 else jnp.logical_not(is_first)
        numbers, places = (jnp.where(is_own, mine, its) for mine, its in zip(own, other))
        total = jnp.zeros((span, node_rows), jnp.bfloat16)
        for k in range(fan):
            ids = jnp.broadcast_to(numbers[k : k + 1, :], (span, node_rows)).astype(jnp.int16)
            total = total + jnp.where(ids == number, one, zero)
        often_ref[nodes, :] = total.T
        counts_ref[nodes, :] = jnp.broadcast_to(places[fan : fan + 1, :], (LANES, LANES)).T
        cot_ref[nodes, :] = jnp.where(is_own, own_cot, other_cot)


def layers_kernel(
    place_ref, got_ref, often_ref, counts_ref, cot_ref, bias_ref, self_ref, neigh_ref,
    hidden_hbm, parts_ref, hidden_ref, left,
):
    node_rows, hid = hidden_ref.shape
    span = 4 * node_rows
    over_rows = (((0,), (0,)), ((), ()))
    is_first = jnp.bitwise_and(place_ref[0], 1) == 0
    got = got_ref[...]
    pre_one = lax.dot_general(
        got[:, :span], got[:, span:], over_rows, preferred_element_type=jnp.float32
    )
    hidden = gelu_parts(pre_one + bias_ref[0:1, :])[0].astype(jnp.bfloat16)
    own = hidden[node_rows : 3 * node_rows]
    summed = jnp.dot(often_ref[...], hidden, preferred_element_type=jnp.float32)
    counts = jnp.concatenate([counts_ref[...]] * (hid // LANES), axis=1)
    agg = (summed / counts).astype(jnp.bfloat16)
    pre_two = jnp.dot(own, self_ref[...], preferred_element_type=jnp.float32)
    pre_two = pre_two + jnp.dot(agg, neigh_ref[...], preferred_element_type=jnp.float32)
    value, slope = gelu_parts(pre_two + bias_ref[1:2, :])
    hidden_ref[...] = jnp.where(is_first, value[:node_rows], value[node_rows:]).astype(jnp.bfloat16)
    copy = pltpu.make_async_copy(hidden_ref, hidden_hbm, left)
    copy.start()
    delta = (cot_ref[...].astype(jnp.float32) * slope).astype(jnp.bfloat16)
    rows = jnp.where(is_first, own, agg)
    grads = lax.dot_general(rows, delta, over_rows, preferred_element_type=jnp.float32)
    bias = jnp.sum(delta.astype(jnp.float32), axis=0, keepdims=True)
    for half in range(2):
        columns = slice(half * LANES, (half + 1) * LANES)
        for part in range(parts_ref.shape[0]):
            parts_ref[part, 4 * half : 4 * half + 4] = grads[
                part * 8 : part * 8 + 8, columns
            ].reshape(4, 2, LANES)
            parts_ref[part, 8, half : half + 1, :] = bias[:, columns]
    copy.wait()


def repeat_kernel(part_ref, out_ref):
    part = jnp.concatenate([part_ref[0:8, :], part_ref[8:16, :]], axis=1).astype(jnp.bfloat16)
    for to in range(out_ref.shape[0]):
        out_ref[to] = part


def widen_kernel(got_ref, total_ref, self_ref, neigh_ref, bias_ref):
    parts, _, rows, _ = got_ref.shape
    for part in range(parts):
        self_ref[part * rows : (part + 1) * rows, :] = got_ref[part, 1].astype(jnp.float32)
        neigh_ref[part * rows : (part + 1) * rows, :] = got_ref[part, 0].astype(jnp.float32)
    bias_ref[...] = jnp.concatenate([total_ref[16:17, :], total_ref[17:18, :]], axis=1)


def from_member(first, size):
    return [(first + i) % size for i in range(size)]


def both_cores(order):
    return [2 * chip + core for chip in order for core in (1, 0)]


def local(
    features,
    neighbours_one,
    counts_one,
    neighbours_two,
    counts_two,
    self_one,
    neigh_one,
    bias_one,
    self_two,
    neigh_two,
    bias_two,
    cotangent,
):
    rows, batch_nodes = features.shape
    pairs, chips, cores = lax.axis_size("pair"), lax.axis_size("chip"), lax.axis_size("core")
    others = lax.axis_size("apart")
    groups = chips * cores
    node_rows = batch_nodes // groups
    hid = self_one.shape[1]
    span = 4 * node_rows
    params = pltpu.CompilerParams(vmem_limit_bytes=VMEM_BYTES)
    group = pairs * chips
    everyone = group * cores
    first_chip = chips // 2 + chips // 8
    first_part = group - chips + first_chip
    feat_order = both_cores(from_member(first_chip, chips))
    part_order = from_member(first_part, group)
    every_order = both_cores(part_order)
    apart_order = sorted(range(others), key=lambda i: (i != others // 2, min(i, others - i)))
    lists = (16, node_rows)
    loads = (
        features, neighbours_one.T, counts_one[None, :], self_one, neigh_one, neighbours_two.T,
        counts_two[None, :], cotangent, bias_one[None, :], bias_two[None, :],
    )
    chunks, send, biases = pl.pallas_call(
        functools.partial(pick_kernel, feat_order),
        out_shape=(
            jax.ShapeDtypeStruct((groups, 2 * rows, span + hid), jnp.bfloat16),
            jax.ShapeDtypeStruct((node_rows + lists[0], hid), jnp.bfloat16),
            jax.ShapeDtypeStruct((2, hid), jnp.float32),
        ),
        in_specs=[pl.BlockSpec(memory_space=pltpu.HBM)] * len(loads),
        scratch_shapes=[pltpu.VMEM(load.shape, load.dtype) for load in loads]
        + [
            pltpu.VMEM((2 * rows, batch_nodes), jnp.float32),
            pltpu.VMEM((4 * rows, batch_nodes), jnp.bfloat16),
            pltpu.VMEM((2 * rows, batch_nodes + 2 * node_rows), jnp.float32),
            pltpu.VMEM(lists, jnp.int32),
            pltpu.SemaphoreType.DMA((len(loads),)),
        ],
        compiler_params=pltpu.CompilerParams(vmem_limit_bytes=PICK_VMEM_BYTES),
        name="pick",
    )(*loads)
    got = lax.all_to_all(
        chunks, ("chip", "core"), 0, 0, tiled=True, axis_index_groups=[feat_order]
    )
    other = lax.ppermute(send, "core", [(0, 1), (1, 0)])
    place = lax.axis_index(("chip", "core"))[None]
    scalar = pl.BlockSpec(memory_space=pltpu.SMEM)
    array = pl.BlockSpec(memory_space=pltpu.VMEM)
    often, counts, cot, biases = pl.pallas_call(
        functools.partial(lists_kernel, neighbours_two.shape[1]),
        out_shape=(
            jax.ShapeDtypeStruct((2 * node_rows, span), jnp.bfloat16),
            jax.ShapeDtypeStruct((2 * node_rows, LANES), jnp.float32),
            jax.ShapeDtypeStruct((2 * node_rows, hid), jnp.bfloat16),
            jax.ShapeDtypeStruct(biases.shape, jnp.float32),
        ),
        in_specs=[scalar, array, array, array],
        compiler_params=params,
        name="lists",
    )(place, send, other, biases)
    hidden_two, parts = pl.pallas_call(
        layers_kernel,
        out_shape=(
            jax.ShapeDtypeStruct((node_rows, hid), jnp.bfloat16),
            jax.ShapeDtypeStruct((group, 9, 2, LANES), jnp.float32),
        ),
        in_specs=[scalar] + [array] * 7,
        out_specs=(pl.BlockSpec(memory_space=pltpu.HBM), array),
        scratch_shapes=[pltpu.VMEM((node_rows, hid), jnp.bfloat16), pltpu.SemaphoreType.DMA],
        compiler_params=params,
        name="layers",
    )(
        place, got.reshape(groups * 2 * rows, span + hid), often, counts, cot, biases, self_two,
        neigh_two,
    )
    inner = lax.all_to_all(
        parts, ("pair", "chip"), 0, 0, tiled=True, axis_index_groups=[part_order]
    ).sum(axis=0)
    spread = jnp.broadcast_to(inner[None], (others,) + inner.shape)
    total = lax.all_to_all(
        spread, "apart", 0, 0, tiled=True, axis_index_groups=[apart_order]
    ).sum(axis=0)
    total = total.reshape(18, LANES) * (1.0 / (batch_nodes * pairs * others))
    spread = pl.pallas_call(
        repeat_kernel,
        out_shape=jax.ShapeDtypeStruct((everyone, hid // group, hid), jnp.bfloat16),
        compiler_params=params,
        name="repeat",
    )(total)
    whole = lax.all_to_all(
        spread, ("pair", "chip", "core"), 0, 0, tiled=True, axis_index_groups=[every_order]
    )
    grad_self, grad_neigh, grad_bias = pl.pallas_call(
        widen_kernel,
        out_shape=(
            jax.ShapeDtypeStruct((hid, hid), jnp.float32),
            jax.ShapeDtypeStruct((hid, hid), jnp.float32),
            jax.ShapeDtypeStruct((1, hid), jnp.float32),
        ),
        compiler_params=params,
        name="widen",
    )(whole.reshape(group, cores, hid // group, hid), total)
    return hidden_two, grad_self, grad_neigh, grad_bias.reshape(hid)


def solution(mesh):
    replicas, groups = mesh.devices.shape
    split = Mesh(
        mesh.devices.reshape(replicas // 2, 2, groups // 2, 2), ("apart", "pair", "chip", "core")
    )
    dp = ("apart", "pair")
    feat = ("chip", "core")
    every = dp + feat
    return jax.shard_map(
        local,
        mesh=split,
        in_specs=(
            P(feat, dp),
            P(dp, None),
            P(dp),
            P(every, None),
            P(every),
            P(feat, None),
            P(feat, None),
            P(),
            P(),
            P(),
            P(),
            P(every, None),
        ),
        out_specs=(P(every, None), P(), P(), P()),
        check_vma=False,
    )
```

```python
import functools
import math

import jax
import jax.numpy as jnp
from jax import lax
from jax.experimental import pallas as pl
from jax.experimental.pallas import tpu as pltpu
from jax.sharding import Mesh
from jax.sharding import PartitionSpec as P

LANES = 128
BY_MATMUL = 8
REACH = 256
DEAD = -64
INNER = math.sqrt(2.0 / math.pi)
CUBIC = 0.044715
VMEM_BYTES = 48 * 1024 * 1024
PICK_VMEM_BYTES = 57_000_000


WITHIN = lax.GatherDimensionNumbers(
    offset_dims=(),
    collapsed_slice_dims=(1,),
    start_index_map=(1,),
    operand_batching_dims=(0,),
    start_indices_batching_dims=(0,),
)


def lane_gather(table, lane):
    return lax.gather(
        table, lane[..., None], WITHIN, (1, 1), mode=lax.GatherScatterMode.PROMISE_IN_BOUNDS
    )


def pick_kernel(
    order, feats_hbm, ids_hbm, counts_hbm, self_hbm, neigh_hbm, ids_two_hbm, counts_two_hbm,
    cot_hbm, bias_one_hbm, bias_two_hbm, out_ref, send_ref, biases_ref,
    feats_ref, ids_ref, counts_ref, self_ref, neigh_ref, ids_two_ref, counts_two_ref, cot_ref,
    bias_one_ref, bias_two_ref, wide, table, sums, lists, arrived,
):
    copies = [
        pltpu.make_async_copy(source, target, arrived.at[i])
        for i, (source, target) in enumerate(
            (
                (feats_hbm, feats_ref),
                (ids_hbm, ids_ref),
                (counts_hbm, counts_ref),
                (self_hbm, self_ref),
                (neigh_hbm, neigh_ref),
                (ids_two_hbm, ids_two_ref),
                (counts_two_hbm, counts_two_ref),
                (cot_hbm, cot_ref),
                (bias_one_hbm, bias_one_ref),
                (bias_two_hbm, bias_two_ref),
            )
        )
    ]
    for copy in copies:
        copy.start()
    rows, nodes = feats_ref.shape
    fan = ids_ref.shape[0]
    blocks = nodes // LANES
    copies[0].wait()
    values = feats_ref[...].astype(jnp.float32)
    wide[0:rows, :] = values
    wide[rows : 2 * rows, :] = values
    table[...] = jnp.concatenate([wide[...]] * 2, axis=0).astype(jnp.bfloat16)
    reaches = nodes // REACH
    flat = jnp.concatenate(
        [values[:, i * REACH : (i + 1) * REACH] for i in range(reaches)], axis=0
    ).astype(jnp.bfloat16)
    for copy in copies[1:3]:
        copy.wait()
    in_reach = lax.broadcasted_iota(jnp.int32, (REACH, LANES), 0).astype(jnp.int16)
    reach_of_row = lax.broadcasted_iota(jnp.int32, (reaches * rows, LANES), 0) // rows
    one, zero = jnp.ones((), jnp.bfloat16), jnp.zeros((), jnp.bfloat16)
    row = lax.broadcasted_iota(jnp.int32, (4 * rows, LANES), 0)
    upper = lax.broadcasted_iota(jnp.int32, (2 * rows, LANES), 0) < rows

    def four_blocks(quad, carry):
        start = pl.multiple_of(quad * 4 * LANES, 4 * LANES)

        def spread(ref, k):
            parts = [
                jnp.broadcast_to(ref[k : k + 1, pl.ds(start + i * LANES, LANES)], row.shape)
                for i in range(4)
            ]
            return jnp.where(
                row < 2 * rows,
                jnp.where(row < rows, parts[0], parts[1]),
                jnp.where(row < 3 * rows, parts[2], parts[3]),
            )

        def by_lanes(k):
            ids = spread(ids_ref, k).astype(jnp.int16)
            lane = jnp.bitwise_and(ids, jnp.int16(LANES - 1))
            level = [
                lane_gather(table[:, j * LANES : (j + 1) * LANES], lane) for j in range(blocks)
            ]
            bit = LANES
            while len(level) > 1:
                odd = jnp.bitwise_and(ids, jnp.int16(bit)) != 0
                level = [
                    jnp.where(odd, level[i + 1], level[i]) for i in range(0, len(level), 2)
                ]
                bit *= 2
            return jnp.where(counts > k, level[0].astype(jnp.float32), 0.0)

        def by_matmul(k, i):
            lanes = pl.ds(start + i * LANES, LANES)
            ids, live = ids_ref[k : k + 1, lanes], counts_ref[0:1, lanes] > k
            place = jnp.broadcast_to(jnp.bitwise_and(ids, REACH - 1), in_reach.shape)
            hot = jnp.where(place.astype(jnp.int16) == in_reach, one, zero)
            found = jnp.dot(flat, hot, preferred_element_type=jnp.float32)
            reach = jnp.where(live, lax.shift_right_logical(ids, REACH.bit_length() - 1), -1)
            found = jnp.where(jnp.broadcast_to(reach, found.shape) == reach_of_row, found, 0.0)
            return jnp.sum(found.reshape(-1, 2 * rows, LANES), axis=0)

        counts = spread(counts_ref, 0)
        total = jnp.zeros(row.shape, jnp.float32)
        pairs = [jnp.zeros(upper.shape, jnp.float32)] * 4
        by_lane = fan - BY_MATMUL
        for k in range(max(by_lane, BY_MATMUL)):
            if k < by_lane:
                total = total + by_lanes(k)
            if k < BY_MATMUL:
                pairs = [pair + by_matmul(by_lane + k, i) for i, pair in enumerate(pairs)]
        pairs = [pair + pltpu.roll(pair, rows, axis=0) for pair in pairs]
        total = total + jnp.concatenate(
            [jnp.where(upper, pairs[i], pairs[i + 1]) for i in (0, 2)], axis=0
        )
        mean = total / counts.astype(jnp.float32)
        for i in range(4):
            half = mean[(i // 2) * 2 * rows : (i // 2 + 1) * 2 * rows]
            if i % 2 == 0:
                half = pltpu.roll(half, rows, axis=0)
            to = pl.multiple_of(start + (i + 1) * LANES, LANES)
            sums[:, pl.ds(to, LANES)] = jnp.where(
                upper, wide[:, pl.ds(start + i * LANES, LANES)], half
            )
        return carry

    lax.fori_loop(0, blocks // 4, four_blocks, 0, unroll=True)
    sums[:, 0:LANES] = sums[:, blocks * LANES : (blocks + 1) * LANES]
    sums[:, (blocks + 1) * LANES :] = sums[:, LANES : 2 * LANES]
    for copy in copies[3:]:
        copy.wait()
    node_rows = cot_ref.shape[0]
    fan_two = ids_two_ref.shape[0]
    lists[...] = jnp.zeros_like(lists)
    lists[0:fan_two, :] = ids_two_ref[...]
    row = lax.broadcasted_iota(jnp.int32, lists.shape, 0)
    counts_two = jnp.broadcast_to(counts_two_ref[...], lists.shape)
    place = jnp.bitwise_and(lists[...], LANES - 1)
    block = jnp.where(row < counts_two, lax.shift_right_logical(lists[...], 7), DEAD)
    place = jnp.where(row == fan_two, counts_two, place)
    send_ref[0:node_rows, :] = cot_ref[...]
    send_ref[node_rows:, 0:LANES] = place.astype(jnp.float32).astype(jnp.bfloat16)
    send_ref[node_rows:, LANES:] = block.astype(jnp.float32).astype(jnp.bfloat16)
    biases_ref[0:1, :] = bias_one_ref[...]
    biases_ref[1:2, :] = bias_two_ref[...]
    weights = jnp.concatenate(
        [self_ref[...].astype(jnp.float32), neigh_ref[...].astype(jnp.float32)], axis=0
    ).astype(jnp.bfloat16)
    for first in range(0, blocks, 2):
        span = sums[:, first * LANES : (first + 4) * LANES].astype(jnp.bfloat16)
        for block in (first, first + 1):
            to = order.index(block)
            out_ref[to, :, 0 : 4 * LANES] = span
            out_ref[to, :, 4 * LANES :] = weights


def gelu_parts(value):
    square = value * value
    half = 0.5 + 0.5 * jnp.tanh(value * (INNER + (INNER * CUBIC) * square))
    gelu = value * half
    slope = half + gelu * (1.0 - half) * (2.0 * INNER + (6.0 * INNER * CUBIC) * square)
    return gelu, slope


def lists_kernel(
    fan, place_ref, own_ref, other_ref, bias_ref, often_ref, counts_ref, cot_ref, biases_ref
):
    span, node_rows = often_ref.shape[1], often_ref.shape[0] // 2
    is_first = jnp.bitwise_and(place_ref[0], 1) == 0
    first_block = lax.shift_right_logical(place_ref[0], 1) * 2 - 1

    def lists_of(ref):
        kept = ref[node_rows:, :].astype(jnp.float32)
        place = kept[:, :LANES]
        numbers = (kept[:, LANES:].astype(jnp.int32) - first_block) * LANES + place.astype(jnp.int32)
        return numbers, place

    biases_ref[...] = bias_ref[...]
    own, other = lists_of(own_ref), lists_of(other_ref)
    number = lax.broadcasted_iota(jnp.int32, (span, node_rows), 0).astype(jnp.int16)
    one, zero = jnp.ones((), jnp.bfloat16), jnp.zeros((), jnp.bfloat16)
    own_cot, other_cot = own_ref[0:node_rows, :], other_ref[0:node_rows, :]
    for block in range(2):
        nodes = slice(block * node_rows, (block + 1) * node_rows)
        is_own = is_first if block == 0 else jnp.logical_not(is_first)
        numbers, places = (jnp.where(is_own, mine, its) for mine, its in zip(own, other))
        total = jnp.zeros((span, node_rows), jnp.bfloat16)
        for k in range(fan):
            ids = jnp.broadcast_to(numbers[k : k + 1, :], (span, node_rows)).astype(jnp.int16)
            total = total + jnp.where(ids == number, one, zero)
        often_ref[nodes, :] = total.T
        counts_ref[nodes, :] = jnp.broadcast_to(places[fan : fan + 1, :], (LANES, LANES)).T
        cot_ref[nodes, :] = jnp.where(is_own, own_cot, other_cot)


def layers_kernel(
    place_ref, got_ref, often_ref, counts_ref, cot_ref, bias_ref, self_ref, neigh_ref,
    hidden_hbm, parts_ref, hidden_ref, left,
):
    node_rows, hid = hidden_ref.shape
    span = 4 * node_rows
    over_rows = (((0,), (0,)), ((), ()))
    is_first = jnp.bitwise_and(place_ref[0], 1) == 0
    got = got_ref[...]
    pre_one = lax.dot_general(
        got[:, :span], got[:, span:], over_rows, preferred_element_type=jnp.float32
    )
    hidden = gelu_parts(pre_one + bias_ref[0:1, :])[0].astype(jnp.bfloat16)
    own = hidden[node_rows : 3 * node_rows]
    summed = jnp.dot(often_ref[...], hidden, preferred_element_type=jnp.float32)
    counts = jnp.concatenate([counts_ref[...]] * (hid // LANES), axis=1)
    agg = (summed / counts).astype(jnp.bfloat16)
    pre_two = jnp.dot(own, self_ref[...], preferred_element_type=jnp.float32)
    pre_two = pre_two + jnp.dot(agg, neigh_ref[...], preferred_element_type=jnp.float32)
    value, slope = gelu_parts(pre_two + bias_ref[1:2, :])
    hidden_ref[...] = jnp.where(is_first, value[:node_rows], value[node_rows:]).astype(jnp.bfloat16)
    copy = pltpu.make_async_copy(hidden_ref, hidden_hbm, left)
    copy.start()
    delta = (cot_ref[...].astype(jnp.float32) * slope).astype(jnp.bfloat16)
    rows = jnp.where(is_first, own, agg)
    grads = lax.dot_general(rows, delta, over_rows, preferred_element_type=jnp.float32)
    bias = jnp.sum(delta.astype(jnp.float32), axis=0, keepdims=True)
    for half in range(2):
        columns = slice(half * LANES, (half + 1) * LANES)
        for part in range(parts_ref.shape[0]):
            parts_ref[part, 4 * half : 4 * half + 4] = grads[
                part * 8 : part * 8 + 8, columns
            ].reshape(4, 2, LANES)
            parts_ref[part, 8, half : half + 1, :] = bias[:, columns]
    copy.wait()


def repeat_kernel(part_ref, out_ref):
    part = jnp.concatenate([part_ref[0:8, :], part_ref[8:16, :]], axis=1).astype(jnp.bfloat16)
    for to in range(out_ref.shape[0]):
        out_ref[to] = part


def widen_kernel(got_ref, total_ref, self_ref, neigh_ref, bias_ref):
    parts, _, rows, _ = got_ref.shape
    for part in range(parts):
        self_ref[part * rows : (part + 1) * rows, :] = got_ref[part, 1].astype(jnp.float32)
        neigh_ref[part * rows : (part + 1) * rows, :] = got_ref[part, 0].astype(jnp.float32)
    bias_ref[...] = jnp.concatenate([total_ref[16:17, :], total_ref[17:18, :]], axis=1)


def from_member(first, size):
    return [(first + i) % size for i in range(size)]


def both_cores(order):
    return [2 * chip + core for chip in order for core in (1, 0)]


def local(
    features,
    neighbours_one,
    counts_one,
    neighbours_two,
    counts_two,
    self_one,
    neigh_one,
    bias_one,
    self_two,
    neigh_two,
    bias_two,
    cotangent,
):
    rows, batch_nodes = features.shape
    pairs, chips, cores = lax.axis_size("pair"), lax.axis_size("chip"), lax.axis_size("core")
    others = lax.axis_size("apart")
    groups = chips * cores
    node_rows = batch_nodes // groups
    hid = self_one.shape[1]
    span = 4 * node_rows
    params = pltpu.CompilerParams(vmem_limit_bytes=VMEM_BYTES)
    group = pairs * chips
    everyone = group * cores
    first_chip = chips // 2 + chips // 8
    first_part = group - chips + first_chip
    feat_order = both_cores(from_member(first_chip, chips))
    part_order = sorted(
        range(group), key=lambda i: (i != first_part, i // chips, (i - first_chip) % chips)
    )
    every_order = both_cores(part_order)
    apart_order = sorted(range(others), key=lambda i: (i != others // 2, min(i, others - i)))
    lists = (16, node_rows)
    loads = (
        features, neighbours_one.T, counts_one[None, :], self_one, neigh_one, neighbours_two.T,
        counts_two[None, :], cotangent, bias_one[None, :], bias_two[None, :],
    )
    chunks, send, biases = pl.pallas_call(
        functools.partial(pick_kernel, feat_order),
        out_shape=(
            jax.ShapeDtypeStruct((groups, 2 * rows, span + hid), jnp.bfloat16),
            jax.ShapeDtypeStruct((node_rows + lists[0], hid), jnp.bfloat16),
            jax.ShapeDtypeStruct((2, hid), jnp.float32),
        ),
        in_specs=[pl.BlockSpec(memory_space=pltpu.HBM)] * len(loads),
        scratch_shapes=[pltpu.VMEM(load.shape, load.dtype) for load in loads]
        + [
            pltpu.VMEM((2 * rows, batch_nodes), jnp.float32),
            pltpu.VMEM((4 * rows, batch_nodes), jnp.bfloat16),
            pltpu.VMEM((2 * rows, batch_nodes + 2 * node_rows), jnp.float32),
            pltpu.VMEM(lists, jnp.int32),
            pltpu.SemaphoreType.DMA((len(loads),)),
        ],
        compiler_params=pltpu.CompilerParams(vmem_limit_bytes=PICK_VMEM_BYTES),
        name="pick",
    )(*loads)
    got = lax.all_to_all(
        chunks, ("chip", "core"), 0, 0, tiled=True, axis_index_groups=[feat_order]
    )
    other = lax.ppermute(send, "core", [(0, 1), (1, 0)])
    place = lax.axis_index(("chip", "core"))[None]
    scalar = pl.BlockSpec(memory_space=pltpu.SMEM)
    array = pl.BlockSpec(memory_space=pltpu.VMEM)
    often, counts, cot, biases = pl.pallas_call(
        functools.partial(lists_kernel, neighbours_two.shape[1]),
        out_shape=(
            jax.ShapeDtypeStruct((2 * node_rows, span), jnp.bfloat16),
            jax.ShapeDtypeStruct((2 * node_rows, LANES), jnp.float32),
            jax.ShapeDtypeStruct((2 * node_rows, hid), jnp.bfloat16),
            jax.ShapeDtypeStruct(biases.shape, jnp.float32),
        ),
        in_specs=[scalar, array, array, array],
        compiler_params=params,
        name="lists",
    )(place, send, other, biases)
    hidden_two, parts = pl.pallas_call(
        layers_kernel,
        out_shape=(
            jax.ShapeDtypeStruct((node_rows, hid), jnp.bfloat16),
            jax.ShapeDtypeStruct((group, 9, 2, LANES), jnp.float32),
        ),
        in_specs=[scalar] + [array] * 7,
        out_specs=(pl.BlockSpec(memory_space=pltpu.HBM), array),
        scratch_shapes=[pltpu.VMEM((node_rows, hid), jnp.bfloat16), pltpu.SemaphoreType.DMA],
        compiler_params=params,
        name="layers",
    )(
        place, got.reshape(groups * 2 * rows, span + hid), often, counts, cot, biases, self_two,
        neigh_two,
    )
    inner = lax.all_to_all(
        parts, ("pair", "chip"), 0, 0, tiled=True, axis_index_groups=[part_order]
    ).sum(axis=0)
    spread = jnp.broadcast_to(inner[None], (others,) + inner.shape)
    total = lax.all_to_all(
        spread, "apart", 0, 0, tiled=True, axis_index_groups=[apart_order]
    ).sum(axis=0)
    total = total.reshape(18, LANES) * (1.0 / (batch_nodes * pairs * others))
    spread = pl.pallas_call(
        repeat_kernel,
        out_shape=jax.ShapeDtypeStruct((everyone, hid // group, hid), jnp.bfloat16),
        compiler_params=params,
        name="repeat",
    )(total)
    whole = lax.all_to_all(
        spread, ("pair", "chip", "core"), 0, 0, tiled=True, axis_index_groups=[every_order]
    )
    grad_self, grad_neigh, grad_bias = pl.pallas_call(
        widen_kernel,
        out_shape=(
            jax.ShapeDtypeStruct((hid, hid), jnp.float32),
            jax.ShapeDtypeStruct((hid, hid), jnp.float32),
            jax.ShapeDtypeStruct((1, hid), jnp.float32),
        ),
        compiler_params=params,
        name="widen",
    )(whole.reshape(group, cores, hid // group, hid), total)
    return hidden_two, grad_self, grad_neigh, grad_bias.reshape(hid)


def solution(mesh):
    replicas, groups = mesh.devices.shape
    split = Mesh(
        mesh.devices.reshape(replicas // 2, 2, groups // 2, 2), ("apart", "pair", "chip", "core")
    )
    dp = ("apart", "pair")
    feat = ("chip", "core")
    every = dp + feat
    return jax.shard_map(
        local,
        mesh=split,
        in_specs=(
            P(feat, dp),
            P(dp, None),
            P(dp),
            P(every, None),
            P(every),
            P(feat, None),
            P(feat, None),
            P(),
            P(),
            P(),
            P(),
            P(every, None),
        ),
        out_specs=(P(every, None), P(), P(), P()),
        check_vma=False,
    )
```

```python
import functools
import math

import jax
import jax.numpy as jnp
from jax import lax
from jax.experimental import pallas as pl
from jax.experimental.pallas import tpu as pltpu
from jax.sharding import Mesh
from jax.sharding import PartitionSpec as P

LANES = 128
BY_MATMUL = 8
REACH = 256
PIECES = 4
DEAD = -64
INNER = math.sqrt(2.0 / math.pi)
CUBIC = 0.044715
VMEM_BYTES = 48 * 1024 * 1024
PICK_VMEM_BYTES = 57_000_000


WITHIN = lax.GatherDimensionNumbers(
    offset_dims=(),
    collapsed_slice_dims=(1,),
    start_index_map=(1,),
    operand_batching_dims=(0,),
    start_indices_batching_dims=(0,),
)


def lane_gather(table, lane):
    return lax.gather(
        table, lane[..., None], WITHIN, (1, 1), mode=lax.GatherScatterMode.PROMISE_IN_BOUNDS
    )


def pick_kernel(
    order, feats_hbm, ids_hbm, counts_hbm, self_hbm, neigh_hbm, ids_two_hbm, counts_two_hbm,
    cot_hbm, bias_one_hbm, bias_two_hbm, out_ref, send_ref, biases_ref,
    feats_ref, ids_ref, counts_ref, self_ref, neigh_ref, ids_two_ref, counts_two_ref, cot_ref,
    bias_one_ref, bias_two_ref, wide, table, sums, lists, arrived,
):
    half_nodes = ids_ref.shape[1] // 2
    early, late = pl.ds(0, half_nodes), pl.ds(half_nodes, half_nodes)
    copies = [
        pltpu.make_async_copy(source, target, arrived.at[i])
        for i, (source, target) in enumerate(
            (
                (feats_hbm, feats_ref),
                (ids_hbm.at[:, early], ids_ref.at[:, early]),
                (counts_hbm, counts_ref),
                (ids_hbm.at[:, late], ids_ref.at[:, late]),
                (self_hbm, self_ref),
                (neigh_hbm, neigh_ref),
                (ids_two_hbm, ids_two_ref),
                (counts_two_hbm, counts_two_ref),
                (cot_hbm, cot_ref),
                (bias_one_hbm, bias_one_ref),
                (bias_two_hbm, bias_two_ref),
            )
        )
    ]
    for copy in copies:
        copy.start()
    rows, nodes = feats_ref.shape
    fan = ids_ref.shape[0]
    blocks = nodes // LANES
    copies[0].wait()
    values = feats_ref[...].astype(jnp.float32)
    wide[0:rows, :] = values
    wide[rows : 2 * rows, :] = values
    table[...] = jnp.concatenate([wide[...]] * 2, axis=0).astype(jnp.bfloat16)
    reaches = nodes // REACH
    flat = jnp.concatenate(
        [values[:, i * REACH : (i + 1) * REACH] for i in range(reaches)], axis=0
    ).astype(jnp.bfloat16)
    for copy in copies[1:3]:
        copy.wait()
    in_reach = lax.broadcasted_iota(jnp.int32, (REACH, LANES), 0).astype(jnp.int16)
    reach_of_row = lax.broadcasted_iota(jnp.int32, (reaches * rows, LANES), 0) // rows
    one, zero = jnp.ones((), jnp.bfloat16), jnp.zeros((), jnp.bfloat16)
    row = lax.broadcasted_iota(jnp.int32, (4 * rows, LANES), 0)
    upper = lax.broadcasted_iota(jnp.int32, (2 * rows, LANES), 0) < rows

    def four_blocks(quad, carry):
        start = pl.multiple_of(quad * 4 * LANES, 4 * LANES)

        def spread(ref, k):
            parts = [
                jnp.broadcast_to(ref[k : k + 1, pl.ds(start + i * LANES, LANES)], row.shape)
                for i in range(4)
            ]
            return jnp.where(
                row < 2 * rows,
                jnp.where(row < rows, parts[0], parts[1]),
                jnp.where(row < 3 * rows, parts[2], parts[3]),
            )

        def by_lanes(k):
            ids = spread(ids_ref, k).astype(jnp.int16)
            lane = jnp.bitwise_and(ids, jnp.int16(LANES - 1))
            level = [
                lane_gather(table[:, j * LANES : (j + 1) * LANES], lane) for j in range(blocks)
            ]
            bit = LANES
            while len(level) > 1:
                odd = jnp.bitwise_and(ids, jnp.int16(bit)) != 0
                level = [
                    jnp.where(odd, level[i + 1], level[i]) for i in range(0, len(level), 2)
                ]
                bit *= 2
            return jnp.where(counts > k, level[0].astype(jnp.float32), 0.0)

        def by_matmul(k, i):
            lanes = pl.ds(start + i * LANES, LANES)
            ids, live = ids_ref[k : k + 1, lanes], counts_ref[0:1, lanes] > k
            place = jnp.broadcast_to(jnp.bitwise_and(ids, REACH - 1), in_reach.shape)
            hot = jnp.where(place.astype(jnp.int16) == in_reach, one, zero)
            found = jnp.dot(flat, hot, preferred_element_type=jnp.float32)
            reach = jnp.where(live, lax.shift_right_logical(ids, REACH.bit_length() - 1), -1)
            found = jnp.where(jnp.broadcast_to(reach, found.shape) == reach_of_row, found, 0.0)
            return jnp.sum(found.reshape(-1, 2 * rows, LANES), axis=0)

        counts = spread(counts_ref, 0)
        total = jnp.zeros(row.shape, jnp.float32)
        pairs = [jnp.zeros(upper.shape, jnp.float32)] * 4
        by_lane = fan - BY_MATMUL
        for k in range(max(by_lane, BY_MATMUL)):
            if k < by_lane:
                total = total + by_lanes(k)
            if k < BY_MATMUL:
                pairs = [pair + by_matmul(by_lane + k, i) for i, pair in enumerate(pairs)]
        pairs = [pair + pltpu.roll(pair, rows, axis=0) for pair in pairs]
        total = total + jnp.concatenate(
            [jnp.where(upper, pairs[i], pairs[i + 1]) for i in (0, 2)], axis=0
        )
        mean = total / counts.astype(jnp.float32)
        for i in range(4):
            half = mean[(i // 2) * 2 * rows : (i // 2 + 1) * 2 * rows]
            if i % 2 == 0:
                half = pltpu.roll(half, rows, axis=0)
            to = pl.multiple_of(start + (i + 1) * LANES, LANES)
            sums[:, pl.ds(to, LANES)] = jnp.where(
                upper, wide[:, pl.ds(start + i * LANES, LANES)], half
            )
        return carry

    lax.fori_loop(0, blocks // 8, four_blocks, 0, unroll=True)
    copies[3].wait()
    lax.fori_loop(blocks // 8, blocks // 4, four_blocks, 0, unroll=True)
    sums[:, 0:LANES] = sums[:, blocks * LANES : (blocks + 1) * LANES]
    sums[:, (blocks + 1) * LANES :] = sums[:, LANES : 2 * LANES]
    for copy in copies[4:]:
        copy.wait()
    node_rows = cot_ref.shape[0]
    fan_two = ids_two_ref.shape[0]
    lists[...] = jnp.zeros_like(lists)
    lists[0:fan_two, :] = ids_two_ref[...]
    row = lax.broadcasted_iota(jnp.int32, lists.shape, 0)
    counts_two = jnp.broadcast_to(counts_two_ref[...], lists.shape)
    place = jnp.bitwise_and(lists[...], LANES - 1)
    block = jnp.where(row < counts_two, lax.shift_right_logical(lists[...], 7), DEAD)
    place = jnp.where(row == fan_two, counts_two, place)
    send_ref[0:node_rows, :] = cot_ref[...]
    send_ref[node_rows:, 0:LANES] = place.astype(jnp.float32).astype(jnp.bfloat16)
    send_ref[node_rows:, LANES:] = block.astype(jnp.float32).astype(jnp.bfloat16)
    biases_ref[0:1, :] = bias_one_ref[...]
    biases_ref[1:2, :] = bias_two_ref[...]
    weights = jnp.concatenate(
        [self_ref[...].astype(jnp.float32), neigh_ref[...].astype(jnp.float32)], axis=0
    ).astype(jnp.bfloat16)
    for first in range(0, blocks, 2):
        span = sums[:, first * LANES : (first + 4) * LANES].astype(jnp.bfloat16)
        for block in (first, first + 1):
            to = order.index(block)
            out_ref[to, :, 0 : 4 * LANES] = span
            out_ref[to, :, 4 * LANES :] = weights


def gelu_parts(value):
    square = value * value
    half = 0.5 + 0.5 * jnp.tanh(value * (INNER + (INNER * CUBIC) * square))
    gelu = value * half
    slope = half + gelu * (1.0 - half) * (2.0 * INNER + (6.0 * INNER * CUBIC) * square)
    return gelu, slope


def lists_kernel(
    fan, place_ref, own_ref, other_ref, bias_ref, often_ref, counts_ref, cot_ref, biases_ref
):
    span, node_rows = often_ref.shape[1], often_ref.shape[0] // 2
    is_first = jnp.bitwise_and(place_ref[0], 1) == 0
    first_block = lax.shift_right_logical(place_ref[0], 1) * 2 - 1

    def lists_of(ref):
        kept = ref[node_rows:, :].astype(jnp.float32)
        place = kept[:, :LANES]
        numbers = (kept[:, LANES:].astype(jnp.int32) - first_block) * LANES + place.astype(jnp.int32)
        return numbers, place

    biases_ref[...] = bias_ref[...]
    own, other = lists_of(own_ref), lists_of(other_ref)
    number = lax.broadcasted_iota(jnp.int32, (span, node_rows), 0).astype(jnp.int16)
    one, zero = jnp.ones((), jnp.bfloat16), jnp.zeros((), jnp.bfloat16)
    own_cot, other_cot = own_ref[0:node_rows, :], other_ref[0:node_rows, :]
    for block in range(2):
        nodes = slice(block * node_rows, (block + 1) * node_rows)
        is_own = is_first if block == 0 else jnp.logical_not(is_first)
        numbers, places = (jnp.where(is_own, mine, its) for mine, its in zip(own, other))
        total = jnp.zeros((span, node_rows), jnp.bfloat16)
        for k in range(fan):
            ids = jnp.broadcast_to(numbers[k : k + 1, :], (span, node_rows)).astype(jnp.int16)
            total = total + jnp.where(ids == number, one, zero)
        often_ref[nodes, :] = total.T
        counts_ref[nodes, :] = jnp.broadcast_to(places[fan : fan + 1, :], (LANES, LANES)).T
        cot_ref[nodes, :] = jnp.where(is_own, own_cot, other_cot)


def layers_kernel(
    place_ref, got_ref, often_ref, counts_ref, cot_ref, bias_ref, self_ref, neigh_ref,
    hidden_hbm, parts_ref, hidden_ref, left,
):
    node_rows, hid = hidden_ref.shape
    span = 4 * node_rows
    over_rows = (((0,), (0,)), ((), ()))
    is_first = jnp.bitwise_and(place_ref[0], 1) == 0
    got = got_ref[...]
    pre_one = lax.dot_general(
        got[:, :span], got[:, span:], over_rows, preferred_element_type=jnp.float32
    )
    hidden = gelu_parts(pre_one + bias_ref[0:1, :])[0].astype(jnp.bfloat16)
    own = hidden[node_rows : 3 * node_rows]
    summed = jnp.dot(often_ref[...], hidden, preferred_element_type=jnp.float32)
    counts = jnp.concatenate([counts_ref[...]] * (hid // LANES), axis=1)
    agg = (summed / counts).astype(jnp.bfloat16)
    pre_two = jnp.dot(own, self_ref[...], preferred_element_type=jnp.float32)
    pre_two = pre_two + jnp.dot(agg, neigh_ref[...], preferred_element_type=jnp.float32)
    value, slope = gelu_parts(pre_two + bias_ref[1:2, :])
    hidden_ref[...] = jnp.where(is_first, value[:node_rows], value[node_rows:]).astype(jnp.bfloat16)
    copy = pltpu.make_async_copy(hidden_ref, hidden_hbm, left)
    copy.start()
    delta = (cot_ref[...].astype(jnp.float32) * slope).astype(jnp.bfloat16)
    rows = jnp.where(is_first, own, agg)
    grads = lax.dot_general(rows, delta, over_rows, preferred_element_type=jnp.float32)
    bias = jnp.sum(delta.astype(jnp.float32), axis=0, keepdims=True)
    for half in range(2):
        columns = slice(half * LANES, (half + 1) * LANES)
        for part in range(parts_ref.shape[0]):
            parts_ref[part, 4 * half : 4 * half + 4] = grads[
                part * 8 : part * 8 + 8, columns
            ].reshape(4, 2, LANES)
            parts_ref[part, 8, half : half + 1, :] = bias[:, columns]
    copy.wait()


def repeat_kernel(part_ref, out_ref):
    part = jnp.concatenate([part_ref[0:8, :], part_ref[8:16, :]], axis=1).astype(jnp.bfloat16)
    for to in range(out_ref.shape[0]):
        out_ref[to] = part


def widen_kernel(got_ref, total_ref, self_hbm, neigh_hbm, bias_ref, self_ref, neigh_ref, left):
    parts, _, rows, _ = got_ref.shape
    each = parts // PIECES
    copies = []
    for piece in range(PIECES):
        span = pl.ds(piece * each * rows, each * rows)
        for core, (kept, out) in enumerate(((self_ref, self_hbm), (neigh_ref, neigh_hbm))):
            for part in range(piece * each, (piece + 1) * each):
                kept[part * rows : (part + 1) * rows, :] = got_ref[part, 1 - core].astype(jnp.float32)
            copies.append(
                pltpu.make_async_copy(kept.at[span, :], out.at[span, :], left.at[2 * piece + core])
            )
            copies[-1].start()
    bias_ref[...] = jnp.concatenate([total_ref[16:17, :], total_ref[17:18, :]], axis=1)
    for copy in copies:
        copy.wait()


def from_member(first, size):
    return [(first + i) % size for i in range(size)]


def both_cores(order):
    return [2 * chip + core for chip in order for core in (1, 0)]


def local(
    features,
    neighbours_one,
    counts_one,
    neighbours_two,
    counts_two,
    self_one,
    neigh_one,
    bias_one,
    self_two,
    neigh_two,
    bias_two,
    cotangent,
):
    rows, batch_nodes = features.shape
    pairs, chips, cores = lax.axis_size("pair"), lax.axis_size("chip"), lax.axis_size("core")
    others = lax.axis_size("apart")
    groups = chips * cores
    node_rows = batch_nodes // groups
    hid = self_one.shape[1]
    span = 4 * node_rows
    params = pltpu.CompilerParams(vmem_limit_bytes=VMEM_BYTES)
    group = pairs * chips
    everyone = group * cores
    first_chip = chips // 2 + chips // 8
    first_part = group - chips + first_chip
    feat_order = both_cores(from_member(first_chip, chips))
    part_order = from_member(first_part, group)
    every_order = both_cores(part_order)
    apart_order = sorted(range(others), key=lambda i: (i != others // 2, min(i, others - i)))
    lists = (16, node_rows)
    loads = (
        features, neighbours_one.T, counts_one[None, :], self_one, neigh_one, neighbours_two.T,
        counts_two[None, :], cotangent, bias_one[None, :], bias_two[None, :],
    )
    chunks, send, biases = pl.pallas_call(
        functools.partial(pick_kernel, feat_order),
        out_shape=(
            jax.ShapeDtypeStruct((groups, 2 * rows, span + hid), jnp.bfloat16),
            jax.ShapeDtypeStruct((node_rows + lists[0], hid), jnp.bfloat16),
            jax.ShapeDtypeStruct((2, hid), jnp.float32),
        ),
        in_specs=[pl.BlockSpec(memory_space=pltpu.HBM)] * len(loads),
        scratch_shapes=[pltpu.VMEM(load.shape, load.dtype) for load in loads]
        + [
            pltpu.VMEM((2 * rows, batch_nodes), jnp.float32),
            pltpu.VMEM((4 * rows, batch_nodes), jnp.bfloat16),
            pltpu.VMEM((2 * rows, batch_nodes + 2 * node_rows), jnp.float32),
            pltpu.VMEM(lists, jnp.int32),
            pltpu.SemaphoreType.DMA((len(loads) + 1,)),
        ],
        compiler_params=pltpu.CompilerParams(vmem_limit_bytes=PICK_VMEM_BYTES),
        name="pick",
    )(*loads)
    got = lax.all_to_all(
        chunks, ("chip", "core"), 0, 0, tiled=True, axis_index_groups=[feat_order]
    )
    other = lax.ppermute(send, "core", [(0, 1), (1, 0)])
    place = lax.axis_index(("chip", "core"))[None]
    scalar = pl.BlockSpec(memory_space=pltpu.SMEM)
    array = pl.BlockSpec(memory_space=pltpu.VMEM)
    often, counts, cot, biases = pl.pallas_call(
        functools.partial(lists_kernel, neighbours_two.shape[1]),
        out_shape=(
            jax.ShapeDtypeStruct((2 * node_rows, span), jnp.bfloat16),
            jax.ShapeDtypeStruct((2 * node_rows, LANES), jnp.float32),
            jax.ShapeDtypeStruct((2 * node_rows, hid), jnp.bfloat16),
            jax.ShapeDtypeStruct(biases.shape, jnp.float32),
        ),
        in_specs=[scalar, array, array, array],
        compiler_params=params,
        name="lists",
    )(place, send, other, biases)
    hidden_two, parts = pl.pallas_call(
        layers_kernel,
        out_shape=(
            jax.ShapeDtypeStruct((node_rows, hid), jnp.bfloat16),
            jax.ShapeDtypeStruct((group, 9, 2, LANES), jnp.float32),
        ),
        in_specs=[scalar] + [array] * 7,
        out_specs=(pl.BlockSpec(memory_space=pltpu.HBM), array),
        scratch_shapes=[pltpu.VMEM((node_rows, hid), jnp.bfloat16), pltpu.SemaphoreType.DMA],
        compiler_params=params,
        name="layers",
    )(
        place, got.reshape(groups * 2 * rows, span + hid), often, counts, cot, biases, self_two,
        neigh_two,
    )
    inner = lax.all_to_all(
        parts, ("pair", "chip"), 0, 0, tiled=True, axis_index_groups=[part_order]
    ).sum(axis=0)
    spread = jnp.broadcast_to(inner[None], (others,) + inner.shape)
    total = lax.all_to_all(
        spread, "apart", 0, 0, tiled=True, axis_index_groups=[apart_order]
    ).sum(axis=0)
    total = total.reshape(18, LANES) * (1.0 / (batch_nodes * pairs * others))
    spread = pl.pallas_call(
        repeat_kernel,
        out_shape=jax.ShapeDtypeStruct((everyone, hid // group, hid), jnp.bfloat16),
        compiler_params=params,
        name="repeat",
    )(total)
    whole = lax.all_to_all(
        spread, ("pair", "chip", "core"), 0, 0, tiled=True, axis_index_groups=[every_order]
    )
    grad_self, grad_neigh, grad_bias = pl.pallas_call(
        widen_kernel,
        out_shape=(
            jax.ShapeDtypeStruct((hid, hid), jnp.float32),
            jax.ShapeDtypeStruct((hid, hid), jnp.float32),
            jax.ShapeDtypeStruct((1, hid), jnp.float32),
        ),
        out_specs=(pl.BlockSpec(memory_space=pltpu.HBM),) * 2 + (array,),
        scratch_shapes=[
            pltpu.VMEM((hid, hid), jnp.float32),
            pltpu.VMEM((hid, hid), jnp.float32),
            pltpu.SemaphoreType.DMA((2 * PIECES,)),
        ],
        compiler_params=params,
        name="widen",
    )(whole.reshape(group, cores, hid // group, hid), total)
    return hidden_two, grad_self, grad_neigh, grad_bias.reshape(hid)


def solution(mesh):
    replicas, groups = mesh.devices.shape
    split = Mesh(
        mesh.devices.reshape(replicas // 2, 2, groups // 2, 2), ("apart", "pair", "chip", "core")
    )
    dp = ("apart", "pair")
    feat = ("chip", "core")
    every = dp + feat
    return jax.shard_map(
        local,
        mesh=split,
        in_specs=(
            P(feat, dp),
            P(dp, None),
            P(dp),
            P(every, None),
            P(every),
            P(feat, None),
            P(feat, None),
            P(),
            P(),
            P(),
            P(),
            P(every, None),
        ),
        out_specs=(P(every, None), P(), P(), P()),
        check_vma=False,
    )
```

```python
import functools
import math

import jax
import jax.numpy as jnp
from jax import lax
from jax.experimental import pallas as pl
from jax.experimental.pallas import tpu as pltpu
from jax.sharding import Mesh
from jax.sharding import PartitionSpec as P

LANES = 128
BY_MATMUL = 8
REACH = 256
DEAD = -64
INNER = math.sqrt(2.0 / math.pi)
CUBIC = 0.044715
VMEM_BYTES = 48 * 1024 * 1024
PICK_VMEM_BYTES = 57_000_000


WITHIN = lax.GatherDimensionNumbers(
    offset_dims=(),
    collapsed_slice_dims=(1,),
    start_index_map=(1,),
    operand_batching_dims=(0,),
    start_indices_batching_dims=(0,),
)


def lane_gather(table, lane):
    return lax.gather(
        table, lane[..., None], WITHIN, (1, 1), mode=lax.GatherScatterMode.PROMISE_IN_BOUNDS
    )


def pick_kernel(
    order, feats_hbm, ids_hbm, counts_hbm, self_hbm, neigh_hbm, ids_two_hbm, counts_two_hbm,
    cot_hbm, bias_one_hbm, bias_two_hbm, out_ref, send_ref, biases_ref,
    feats_ref, ids_ref, counts_ref, self_ref, neigh_ref, ids_two_ref, counts_two_ref, cot_ref,
    bias_one_ref, bias_two_ref, wide, table, sums, lists, arrived,
):
    copies = [
        pltpu.make_async_copy(source, target, arrived.at[i])
        for i, (source, target) in enumerate(
            (
                (feats_hbm, feats_ref),
                (ids_hbm, ids_ref),
                (counts_hbm, counts_ref),
                (self_hbm, self_ref),
                (neigh_hbm, neigh_ref),
                (ids_two_hbm, ids_two_ref),
                (counts_two_hbm, counts_two_ref),
                (cot_hbm, cot_ref),
                (bias_one_hbm, bias_one_ref),
                (bias_two_hbm, bias_two_ref),
            )
        )
    ]
    for copy in copies:
        copy.start()
    rows, nodes = feats_ref.shape
    fan = ids_ref.shape[0]
    blocks = nodes // LANES
    copies[0].wait()
    values = feats_ref[...].astype(jnp.float32)
    wide[0:rows, :] = values
    wide[rows : 2 * rows, :] = values
    table[...] = jnp.concatenate([wide[...]] * 2, axis=0).astype(jnp.bfloat16)
    reaches = nodes // REACH
    flat = jnp.concatenate(
        [values[:, i * REACH : (i + 1) * REACH] for i in range(reaches)], axis=0
    ).astype(jnp.bfloat16)
    for copy in copies[1:3]:
        copy.wait()
    in_reach = lax.broadcasted_iota(jnp.int32, (REACH, LANES), 0).astype(jnp.int16)
    reach_of_row = lax.broadcasted_iota(jnp.int32, (reaches * rows, LANES), 0) // rows
    one, zero = jnp.ones((), jnp.bfloat16), jnp.zeros((), jnp.bfloat16)
    row = lax.broadcasted_iota(jnp.int32, (4 * rows, LANES), 0)
    upper = lax.broadcasted_iota(jnp.int32, (2 * rows, LANES), 0) < rows

    def four_blocks(quad, carry):
        start = pl.multiple_of(quad * 4 * LANES, 4 * LANES)

        def spread(ref, k):
            parts = [
                jnp.broadcast_to(ref[k : k + 1, pl.ds(start + i * LANES, LANES)], row.shape)
                for i in range(4)
            ]
            return jnp.where(
                row < 2 * rows,
                jnp.where(row < rows, parts[0], parts[1]),
                jnp.where(row < 3 * rows, parts[2], parts[3]),
            )

        def by_lanes(k):
            ids = spread(ids_ref, k).astype(jnp.int16)
            lane = jnp.bitwise_and(ids, jnp.int16(LANES - 1))
            level = [
                lane_gather(table[:, j * LANES : (j + 1) * LANES], lane) for j in range(blocks)
            ]
            bit = LANES
            while len(level) > 1:
                odd = jnp.bitwise_and(ids, jnp.int16(bit)) != 0
                level = [
                    jnp.where(odd, level[i + 1], level[i]) for i in range(0, len(level), 2)
                ]
                bit *= 2
            return jnp.where(counts > k, level[0].astype(jnp.float32), 0.0)

        def by_matmul(k, i):
            lanes = pl.ds(start + i * LANES, LANES)
            ids, live = ids_ref[k : k + 1, lanes], counts_ref[0:1, lanes] > k
            place = jnp.broadcast_to(jnp.bitwise_and(ids, REACH - 1), in_reach.shape)
            hot = jnp.where(place.astype(jnp.int16) == in_reach, one, zero)
            found = jnp.dot(flat, hot, preferred_element_type=jnp.float32)
            reach = jnp.where(live, lax.shift_right_logical(ids, REACH.bit_length() - 1), -1)
            found = jnp.where(jnp.broadcast_to(reach, found.shape) == reach_of_row, found, 0.0)
            return jnp.sum(found.reshape(-1, 2 * rows, LANES), axis=0)

        counts = spread(counts_ref, 0)
        total = jnp.zeros(row.shape, jnp.float32)
        pairs = [jnp.zeros(upper.shape, jnp.float32)] * 4
        by_lane = fan - BY_MATMUL
        for k in range(max(by_lane, BY_MATMUL)):
            if k < by_lane:
                total = total + by_lanes(k)
            if k < BY_MATMUL:
                pairs = [pair + by_matmul(by_lane + k, i) for i, pair in enumerate(pairs)]
        pairs = [pair + pltpu.roll(pair, rows, axis=0) for pair in pairs]
        total = total + jnp.concatenate(
            [jnp.where(upper, pairs[i], pairs[i + 1]) for i in (0, 2)], axis=0
        )
        mean = total / counts.astype(jnp.float32)
        for i in range(4):
            half = mean[(i // 2) * 2 * rows : (i // 2 + 1) * 2 * rows]
            if i % 2 == 0:
                half = pltpu.roll(half, rows, axis=0)
            to = pl.multiple_of(start + (i + 1) * LANES, LANES)
            sums[:, pl.ds(to, LANES)] = jnp.where(
                upper, wide[:, pl.ds(start + i * LANES, LANES)], half
            )
        return carry

    lax.fori_loop(0, blocks // 4, four_blocks, 0, unroll=True)
    sums[:, 0:LANES] = sums[:, blocks * LANES : (blocks + 1) * LANES]
    sums[:, (blocks + 1) * LANES :] = sums[:, LANES : 2 * LANES]
    for copy in copies[3:]:
        copy.wait()
    node_rows = cot_ref.shape[0]
    fan_two = ids_two_ref.shape[0]
    lists[...] = jnp.zeros_like(lists)
    lists[0:fan_two, :] = ids_two_ref[...]
    row = lax.broadcasted_iota(jnp.int32, lists.shape, 0)
    counts_two = jnp.broadcast_to(counts_two_ref[...], lists.shape)
    place = jnp.bitwise_and(lists[...], LANES - 1)
    block = jnp.where(row < counts_two, lax.shift_right_logical(lists[...], 7), DEAD)
    place = jnp.where(row == fan_two, counts_two, place)
    send_ref[0:node_rows, :] = cot_ref[...]
    send_ref[node_rows:, 0:LANES] = place.astype(jnp.float32).astype(jnp.bfloat16)
    send_ref[node_rows:, LANES:] = block.astype(jnp.float32).astype(jnp.bfloat16)
    biases_ref[0:1, :] = bias_one_ref[...]
    biases_ref[1:2, :] = bias_two_ref[...]
    weights = jnp.concatenate(
        [self_ref[...].astype(jnp.float32), neigh_ref[...].astype(jnp.float32)], axis=0
    ).astype(jnp.bfloat16)
    for first in range(0, blocks, 2):
        span = sums[:, first * LANES : (first + 4) * LANES].astype(jnp.bfloat16)
        for block in (first, first + 1):
            to = order.index(block)
            out_ref[to, :, 0 : 4 * LANES] = span
            out_ref[to, :, 4 * LANES :] = weights


def gelu_parts(value):
    square = value * value
    half = 0.5 + 0.5 * jnp.tanh(value * (INNER + (INNER * CUBIC) * square))
    gelu = value * half
    slope = half + gelu * (1.0 - half) * (2.0 * INNER + (6.0 * INNER * CUBIC) * square)
    return gelu, slope


def lists_kernel(
    fan, place_ref, own_ref, other_ref, bias_ref, often_ref, counts_ref, cot_ref, biases_ref
):
    span, node_rows = often_ref.shape[1], often_ref.shape[0] // 2
    is_first = jnp.bitwise_and(place_ref[0], 1) == 0
    first_block = lax.shift_right_logical(place_ref[0], 1) * 2 - 1

    def lists_of(ref):
        kept = ref[node_rows:, :].astype(jnp.float32)
        place = kept[:, :LANES]
        numbers = (kept[:, LANES:].astype(jnp.int32) - first_block) * LANES + place.astype(jnp.int32)
        return numbers, place

    biases_ref[...] = bias_ref[...]
    own, other = lists_of(own_ref), lists_of(other_ref)
    number = lax.broadcasted_iota(jnp.int32, (span, node_rows), 0).astype(jnp.int16)
    one, zero = jnp.ones((), jnp.bfloat16), jnp.zeros((), jnp.bfloat16)
    own_cot, other_cot = own_ref[0:node_rows, :], other_ref[0:node_rows, :]
    for block in range(2):
        nodes = slice(block * node_rows, (block + 1) * node_rows)
        is_own = is_first if block == 0 else jnp.logical_not(is_first)
        numbers, places = (jnp.where(is_own, mine, its) for mine, its in zip(own, other))
        total = jnp.zeros((span, node_rows), jnp.bfloat16)
        for k in range(fan):
            ids = jnp.broadcast_to(numbers[k : k + 1, :], (span, node_rows)).astype(jnp.int16)
            total = total + jnp.where(ids == number, one, zero)
        often_ref[nodes, :] = total.T
        counts_ref[nodes, :] = jnp.broadcast_to(places[fan : fan + 1, :], (LANES, LANES)).T
        cot_ref[nodes, :] = jnp.where(is_own, own_cot, other_cot)


def layers_kernel(
    place_ref, got_ref, often_ref, counts_ref, cot_ref, bias_ref, self_ref, neigh_ref,
    hidden_hbm, parts_ref, hidden_ref, left,
):
    node_rows, hid = hidden_ref.shape
    span = 4 * node_rows
    over_rows = (((0,), (0,)), ((), ()))
    is_first = jnp.bitwise_and(place_ref[0], 1) == 0
    got = got_ref[...]
    pre_one = lax.dot_general(
        got[:, :span], got[:, span:], over_rows, preferred_element_type=jnp.float32
    )
    hidden = gelu_parts(pre_one + bias_ref[0:1, :])[0].astype(jnp.bfloat16)
    own = hidden[node_rows : 3 * node_rows]
    summed = jnp.dot(often_ref[...], hidden, preferred_element_type=jnp.float32)
    counts = jnp.concatenate([counts_ref[...]] * (hid // LANES), axis=1)
    agg = (summed / counts).astype(jnp.bfloat16)
    pre_two = jnp.dot(own, self_ref[...], preferred_element_type=jnp.float32)
    pre_two = pre_two + jnp.dot(agg, neigh_ref[...], preferred_element_type=jnp.float32)
    value, slope = gelu_parts(pre_two + bias_ref[1:2, :])
    hidden_ref[...] = jnp.where(is_first, value[:node_rows], value[node_rows:]).astype(jnp.bfloat16)
    copy = pltpu.make_async_copy(hidden_ref, hidden_hbm, left)
    copy.start()
    delta = (cot_ref[...].astype(jnp.float32) * slope).astype(jnp.bfloat16)
    rows = jnp.where(is_first, own, agg)
    grads = lax.dot_general(rows, delta, over_rows, preferred_element_type=jnp.float32)
    bias = jnp.sum(delta.astype(jnp.float32), axis=0, keepdims=True)
    for half in range(2):
        columns = slice(half * LANES, (half + 1) * LANES)
        for part in range(parts_ref.shape[0]):
            parts_ref[part, 4 * half : 4 * half + 4] = grads[
                part * 8 : part * 8 + 8, columns
            ].reshape(4, 2, LANES)
            parts_ref[part, 8, half : half + 1, :] = bias[:, columns]
    copy.wait()


def repeat_kernel(part_ref, out_ref):
    part = jnp.concatenate([part_ref[0:8, :], part_ref[8:16, :]], axis=1).astype(jnp.bfloat16)
    for to in range(out_ref.shape[0]):
        out_ref[to] = part


def widen_kernel(got_ref, total_ref, self_ref, neigh_ref, bias_ref):
    parts, _, rows, _ = got_ref.shape
    for part in range(parts):
        self_ref[part * rows : (part + 1) * rows, :] = got_ref[part, 1].astype(jnp.float32)
        neigh_ref[part * rows : (part + 1) * rows, :] = got_ref[part, 0].astype(jnp.float32)
    bias_ref[...] = jnp.concatenate([total_ref[16:17, :], total_ref[17:18, :]], axis=1)


def from_member(first, size):
    return [(first + i) % size for i in range(size)]


def both_cores(order):
    return [2 * chip + core for chip in order for core in (1, 0)]


def local(
    features,
    neighbours_one,
    counts_one,
    neighbours_two,
    counts_two,
    self_one,
    neigh_one,
    bias_one,
    self_two,
    neigh_two,
    bias_two,
    cotangent,
):
    rows, batch_nodes = features.shape
    pairs, chips, cores = lax.axis_size("pair"), lax.axis_size("chip"), lax.axis_size("core")
    others = lax.axis_size("apart")
    groups = chips * cores
    node_rows = batch_nodes // groups
    hid = self_one.shape[1]
    span = 4 * node_rows
    params = pltpu.CompilerParams(vmem_limit_bytes=VMEM_BYTES)
    group = pairs * chips
    everyone = group * cores
    first_chip = chips // 2 + chips // 8
    first_part = group - chips + first_chip
    feat_order = both_cores(from_member(first_chip, chips))
    part_order = from_member(first_part, group)
    every_order = both_cores(part_order)
    apart_order = sorted(range(others), key=lambda i: (i != others // 2, min(i, others - i)))
    lists = (16, node_rows)
    loads = (
        features, neighbours_one.T, counts_one[None, :], self_one, neigh_one, neighbours_two.T,
        counts_two[None, :], cotangent, bias_one[None, :], bias_two[None, :],
    )
    chunks, send, biases = pl.pallas_call(
        functools.partial(pick_kernel, feat_order),
        out_shape=(
            jax.ShapeDtypeStruct((groups, 2 * rows, span + hid), jnp.bfloat16),
            jax.ShapeDtypeStruct((node_rows + lists[0], hid), jnp.bfloat16),
            jax.ShapeDtypeStruct((2, hid), jnp.float32),
        ),
        in_specs=[pl.BlockSpec(memory_space=pltpu.HBM)] * len(loads),
        scratch_shapes=[pltpu.VMEM(load.shape, load.dtype) for load in loads]
        + [
            pltpu.VMEM((2 * rows, batch_nodes), jnp.float32),
            pltpu.VMEM((4 * rows, batch_nodes), jnp.bfloat16),
            pltpu.VMEM((2 * rows, batch_nodes + 2 * node_rows), jnp.float32),
            pltpu.VMEM(lists, jnp.int32),
            pltpu.SemaphoreType.DMA((len(loads),)),
        ],
        compiler_params=pltpu.CompilerParams(vmem_limit_bytes=PICK_VMEM_BYTES),
        name="pick",
    )(*loads)
    got = lax.all_to_all(
        chunks, ("chip", "core"), 0, 0, tiled=True, axis_index_groups=[feat_order]
    )
    other = lax.ppermute(send, "core", [(0, 1), (1, 0)])
    place = lax.axis_index(("chip", "core"))[None]
    scalar = pl.BlockSpec(memory_space=pltpu.SMEM)
    array = pl.BlockSpec(memory_space=pltpu.VMEM)
    often, counts, cot, biases = pl.pallas_call(
        functools.partial(lists_kernel, neighbours_two.shape[1]),
        out_shape=(
            jax.ShapeDtypeStruct((2 * node_rows, span), jnp.bfloat16),
            jax.ShapeDtypeStruct((2 * node_rows, LANES), jnp.float32),
            jax.ShapeDtypeStruct((2 * node_rows, hid), jnp.bfloat16),
            jax.ShapeDtypeStruct(biases.shape, jnp.float32),
        ),
        in_specs=[scalar, array, array, array],
        compiler_params=params,
        name="lists",
    )(place, send, other, biases)
    hidden_two, parts = pl.pallas_call(
        layers_kernel,
        out_shape=(
            jax.ShapeDtypeStruct((node_rows, hid), jnp.bfloat16),
            jax.ShapeDtypeStruct((group, 9, 2, LANES), jnp.float32),
        ),
        in_specs=[scalar] + [array] * 7,
        out_specs=(pl.BlockSpec(memory_space=pltpu.HBM), array),
        scratch_shapes=[pltpu.VMEM((node_rows, hid), jnp.bfloat16), pltpu.SemaphoreType.DMA],
        compiler_params=params,
        name="layers",
    )(
        place, got.reshape(groups * 2 * rows, span + hid), often, counts, cot, biases, self_two,
        neigh_two,
    )
    inner = lax.all_to_all(
        parts, ("pair", "chip"), 0, 0, tiled=True, axis_index_groups=[part_order]
    ).sum(axis=0)
    spread = jnp.broadcast_to(inner[None], (others,) + inner.shape)
    total = lax.all_to_all(
        spread, "apart", 0, 0, tiled=True, axis_index_groups=[apart_order]
    ).sum(axis=0)
    total = total.reshape(18, LANES) * (1.0 / (batch_nodes * pairs * others))
    spread = pl.pallas_call(
        repeat_kernel,
        out_shape=jax.ShapeDtypeStruct((everyone, hid // group, hid), jnp.bfloat16),
        compiler_params=params,
        name="repeat",
    )(total)
    whole = lax.all_to_all(
        spread, ("pair", "chip", "core"), 0, 0, tiled=True, axis_index_groups=[every_order]
    )
    grad_self, grad_neigh, grad_bias = pl.pallas_call(
        widen_kernel,
        out_shape=(
            jax.ShapeDtypeStruct((hid, hid), jnp.float32),
            jax.ShapeDtypeStruct((hid, hid), jnp.float32),
            jax.ShapeDtypeStruct((1, hid), jnp.float32),
        ),
        compiler_params=params,
        name="widen",
    )(whole.reshape(group, cores, hid // group, hid), total)
    return hidden_two, grad_self, grad_neigh, grad_bias.reshape(hid)


def solution(mesh):
    replicas, groups = mesh.devices.shape
    split = Mesh(
        mesh.devices.reshape(replicas // 2, 2, groups // 2, 2), ("apart", "pair", "chip", "core")
    )
    dp = ("apart", "pair")
    feat = ("chip", "core")
    every = dp + feat
    return jax.shard_map(
        local,
        mesh=split,
        in_specs=(
            P(feat, dp),
            P(dp, None),
            P(dp),
            P(every, None),
            P(every),
            P(feat, None),
            P(feat, None),
            P(),
            P(),
            P(),
            P(),
            P(every, None),
        ),
        out_specs=(P(every, None), P(), P(), P()),
        check_vma=False,
    )
```
